32 devices in a mesh: conv: 2 (over y), ctx: 4 (over x, core), head: 4 (over z).
Axes of the slice: x: 2, y: 2, z: 4, core: 2. Of those that a mesh axis runs over, the one named last changes fastest.
Arguments:
- queries: bfloat16 [512, 64, 128], P(('conv', 'ctx'), 'head'), parts along dimension 0, may hold values from -240 to 240, as said below
- new_keys: bfloat16 [512, 8, 128], P(('conv', 'ctx'), 'head'), parts along dimension 0, may hold values from -8 to 8
- new_values: bfloat16 [512, 8, 128], P(('conv', 'ctx'), 'head'), parts along dimension 0, may hold values from -18 to 18
- cache_keys: bfloat16 [16384, 8, 128], P(('conv', 'ctx'), 'head'), parts along dimension 0, may hold values from -6 to 6
- cache_values: bfloat16 [16384, 8, 128], P(('conv', 'ctx'), 'head'), parts along dimension 0, may hold values from -18 to 18
- cache_len: int32 [2], P('conv'), parts along dimension 0, may hold values from 4097 to 8192
Outputs:
- attended: bfloat16 [512, 64, 128], P(('conv', 'ctx'), 'head'), parts along dimension 0
The draws below stay inside these ranges and needn't reach their ends.
There are 2 independent parts, one for each index of `conv`. The reference program is written for one: setup_inputs(seed, part) draws one part's arguments, and reference() takes and returns one part's arrays. A program takes and returns all parts, laid end to end along the dimension named above; each array names one. Nothing has to cross between parts.
Inputs may be any that keep to these rules, and one draw needn't show every extreme that they name: `queries`: each query row is a row of independent entries times a row scale.
All inputs are finite; a program needn't handle non-finite values.
Results may differ from the reference program's by a relative error of at most 0.01.
Values may be sent and summed in bfloat16 or wider, within the bound.
No kernel may reach another device: no remote copies, remote signals or barrier semaphores. Data moves between devices by JAX's collectives and lax.ppermute only.
A program may use at most 64 MiB of HBM per device.

```python
import math
import jax
import jax.numpy as jnp
from jax import lax

HQ = 64
KVH = 8
HD = 128
CACHE_DEV = 2048
TNEW = 256
CACHE = 8192
N_CTX = 4


def draw_queries(key, part):
    first, second = jax.random.split(jax.random.fold_in(key, 17), 2)
    base = jnp.clip(jax.random.normal(first, (TNEW, HQ, HD), jnp.float32), -4.0, 4.0)
    scale = jnp.exp(jax.random.uniform(second, (TNEW, HQ, 1), jnp.float32, jnp.log(1.5), jnp.log(3.2)))
    return (base * scale).astype(jnp.bfloat16)


def block_levels(stream_key, shape, pieces, least, top_value):
    def one(position, shards_of):
        draws = jax.random.uniform(jax.random.fold_in(jax.random.fold_in(stream_key, 6), position), (shards_of,), jnp.float32, least / len(pieces), top_value / len(pieces))
        return jnp.repeat(jnp.exp(draws), shape[position] // shards_of).reshape((-1,) + (1,) * (len(shape) - position - 1))

    gain = one(*pieces[0])
    for cut in pieces[1:]:
        gain = gain * one(*cut)
    return gain


def scatter_about(own_key, shape, scale, most, pieces=(), kind=jnp.bfloat16):
    values = scale * jax.random.normal(own_key, shape, jnp.float32)
    if pieces:
        values = values * block_levels(own_key, shape, pieces, -0.22, 0.18)
    return jnp.clip(values, -most, most).astype(kind)


def setup_inputs(seed: int = 0, part: int = 0) -> dict:
    arg_keys = jax.random.split(jax.random.key(seed), 7)
    part_keys = jax.random.split(jax.random.fold_in(arg_keys[6], part), 7)
    return {
        "queries": draw_queries(jax.random.fold_in(jax.random.fold_in(arg_keys[6], part), 71), part),
        "new_keys": scatter_about(part_keys[1], (TNEW, KVH, HD), 1.6, 8.0, ((0, 4), (1, 4))),
        "new_values": scatter_about(part_keys[2], (TNEW, KVH, HD), 3.0, 18.0, ((0, 4), (1, 4))),
        "cache_keys": scatter_about(part_keys[3], (CACHE, KVH, HD), 1.0, 6.0, ((0, 4), (1, 4))),
        "cache_values": scatter_about(part_keys[4], (CACHE, KVH, HD), 3.0, 18.0, ((0, 4), (1, 4))),
        "cache_len": jax.random.randint(part_keys[5], (1,), CACHE // 2 + 1, CACHE + 1).astype(jnp.int32),
    }


def partial_attend(query_rows, keys, values, valid):
    scores = jnp.einsum('tkgd,skd->tkgs', query_rows.astype(jnp.float32), keys.astype(jnp.float32)) * (1.0 / math.sqrt(HD))
    mask = valid[:, None, None, :]
    scores = jnp.where(mask, scores, jnp.float32(-1e+30))
    peak = lax.optimization_barrier(jnp.max(scores, axis=-1))
    expo = jnp.where(mask, jnp.exp(scores - peak[..., None]), jnp.float32(0.0))
    total = lax.optimization_barrier(jnp.sum(expo, axis=-1))
    rounded = lax.optimization_barrier(expo.astype(jnp.bfloat16)).astype(jnp.float32)
    out = jnp.einsum('tkgs,skd->tkgd', rounded, values.astype(jnp.float32))
    return (out, peak, total)

def reference(queries, new_keys, new_values, cache_keys, cache_values, cache_len):
    group = HQ // KVH
    grouped = queries.reshape(TNEW, KVH, group, HD)
    limit = cache_len[0]

    def one_shard(index):
        start = (index * CACHE_DEV).astype(jnp.int32)
        keys = lax.dynamic_slice_in_dim(cache_keys, start, CACHE_DEV, 0)
        values = lax.dynamic_slice_in_dim(cache_values, start, CACHE_DEV, 0)
        slot_ids = start + jnp.arange(CACHE_DEV, dtype=jnp.int32)
        out, peak, total = partial_attend(grouped, keys, values, (slot_ids < limit)[None, :])
        floored = jnp.maximum(total, 1.0)
        norm = lax.optimization_barrier((out / floored[..., None]).astype(jnp.bfloat16)).astype(jnp.float32)
        return (norm, peak + jnp.log(floored))
    norms, lses = lax.map(one_shard, jnp.arange(N_CTX, dtype=jnp.int32))
    token_ids = jnp.arange(TNEW, dtype=jnp.int32)
    causal = token_ids[None, :] <= token_ids[:, None]
    turn_out, turn_max, turn_total = partial_attend(grouped, new_keys, new_values, causal)
    top = jnp.maximum(lax.optimization_barrier(jnp.max(lses, axis=0)), turn_max)
    shard_scale = jnp.exp(lses - top[None])
    turn_scale = jnp.exp(turn_max - top)
    numer = lax.optimization_barrier(jnp.sum(norms * shard_scale[..., None], axis=0)) + turn_out * turn_scale[..., None]
    denom = lax.optimization_barrier(jnp.sum(shard_scale, axis=0)) + turn_total * turn_scale
    result = numer / denom[..., None]
    return result.reshape(TNEW, HQ, HD).astype(jnp.bfloat16)
```

```python
import functools
import math

import jax
import jax.numpy as jnp
from jax import lax
from jax.experimental import pallas as pl
from jax.experimental.pallas import tpu as pltpu
from jax.sharding import PartitionSpec as P

NEG_FILL = -1e30
LOG2E = 1.4426950408889634
LN2 = 0.6931471805599453
VMEM = pl.BlockSpec(memory_space=pltpu.VMEM)
SMEM = pl.BlockSpec(memory_space=pltpu.SMEM)
F32 = jnp.float32
BF16 = jnp.bfloat16


def params():
    return pltpu.CompilerParams(vmem_limit_bytes=40 * 2**20)


def pack_rows(column):
    rows = column.shape[0]
    flat = jnp.transpose(jnp.broadcast_to(column, (rows, 128)))[0:1, :]
    return jnp.concatenate([flat[:, i * 128 : (i + 1) * 128] for i in range(rows // 128)], axis=0)


def spread_rows(packed):
    return jnp.concatenate(
        [jnp.transpose(jnp.broadcast_to(packed[i : i + 1, :], (128, 128))) for i in range(packed.shape[0])], axis=0
    )


def prepare(info, k_ref, v_ref, nk_ref, nv_ref, keys, values):
    slots, kv, hd = k_ref.shape
    fresh = nk_ref.shape[0]
    filled = info[0]
    ok = lax.broadcasted_iota(jnp.int32, (slots, hd), 0) < filled
    all_k = jnp.swapaxes(k_ref[...], 0, 1)
    all_v = jnp.swapaxes(v_ref[...], 0, 1)
    new_k = jnp.swapaxes(nk_ref[...], 0, 1)
    new_v = jnp.swapaxes(nv_ref[...], 0, 1)
    ones = jnp.where(ok, 1.0, 0.0).astype(BF16)
    for h in range(kv):
        fill = jnp.where(filled > 0, all_k[h, 0:1, :].astype(F32), new_k[h, 0:1, :].astype(F32))
        keys[h, 0:slots] = jnp.where(ok, all_k[h].astype(F32), fill).astype(BF16)
        keys[h, slots:] = new_k[h]
        values[h, 0:slots, 0:hd] = jnp.where(ok, all_v[h].astype(F32), 0.0).astype(BF16)
        values[h, 0:slots, hd:] = ones
        values[h, slots:, 0:hd] = new_v[h]
        values[h, slots:, hd:] = jnp.ones((fresh, hd), BF16)


def attend(offset, q_ref, keys, values, o_ref, l_ref):
    tokens, heads, hd = q_ref.shape
    kv, span, _ = keys.shape
    group = heads // kv
    fresh = tokens
    slots = span - fresh
    scale = LOG2E / math.sqrt(hd)
    tile = min(tokens, 256 // group)
    rows = tile * group
    per = rows // 128
    for h in range(kv):
        for r in range(tokens // tile):
            q = q_ref[r * tile : (r + 1) * tile, h * group : (h + 1) * group, :].reshape(rows, hd)
            nt = (((1,), (1,)), ((), ()))
            s = lax.dot_general(q, keys[h, 0:slots], nt, preferred_element_type=F32)
            s2 = lax.dot_general(q, keys[h, slots:], nt, preferred_element_type=F32)
            token = r * tile + lax.broadcasted_iota(jnp.int32, (rows, fresh), 0) // group
            seen = token + offset >= lax.broadcasted_iota(jnp.int32, (rows, fresh), 1)
            s2 = jnp.where(seen, s2, NEG_FILL)
            peak = jnp.maximum(jnp.max(s, axis=-1, keepdims=True), jnp.max(s2, axis=-1, keepdims=True))
            w = jnp.exp2((s - peak) * scale).astype(BF16)
            w2 = jnp.where(seen, jnp.exp2((s2 - peak) * scale), 0.0).astype(BF16)
            out = jnp.dot(w, values[h, 0:slots], preferred_element_type=F32)
            out = out + jnp.dot(w2, values[h, slots:], preferred_element_type=F32)
            total = out[:, hd:]
            norm = out[:, 0:hd] / jnp.maximum(total, 1.0)
            o_ref[r * tile : (r + 1) * tile, h * group : (h + 1) * group, :] = norm.astype(BF16).reshape(tile, group, hd)
            total = total[:, 0:1]
            lse = jnp.where(total > 0.0, peak * (1.0 / math.sqrt(hd)) + jnp.log(jnp.maximum(total, 1.0)), NEG_FILL)
            at = h * (tokens * group // 128) + r * per
            l_ref[at : at + per, :] = pack_rows(lse)


def blend(group, parts, o_ref, l_ref=None):
    tokens, heads, hd = o_ref.shape
    lses = [l[...] for _, l in parts]
    top = functools.reduce(jnp.maximum, lses)
    scales = [jnp.exp(l - top) for l in lses]
    total = functools.reduce(jnp.add, scales)
    if l_ref is not None:
        l_ref[...] = jnp.where(top > 0.5 * NEG_FILL, top + jnp.log(total), NEG_FILL)
    inv = 1.0 / total
    kv = heads // group
    n = tokens * group // 128
    for h in range(kv):
        acc = None
        for (norm, _), s in zip(parts, scales):
            wide = spread_rows((s * inv)[h * n : (h + 1) * n, :])
            term = norm[:, h * group : (h + 1) * group, :].reshape(tokens * group, hd).astype(F32) * wide
            acc = term if acc is None else acc + term
        o_ref[:, h * group : (h + 1) * group, :] = acc.astype(BF16).reshape(tokens, group, hd)


def first_kernel(info, qa, qb, k, v, nk, nv, oa, la, ob, lb, keys, values):
    prepare(info, k, v, nk, nv, keys, values)
    attend(info[1], qa, keys, values, oa, la)
    attend(info[2], qb, keys, values, ob, lb)


def next_kernel(info, qa, keys, values, oa, la):
    attend(info[1], qa, keys, values, oa, la)


def blend2_kernel(group, a, la, b, lb, o, l):
    blend(group, [(a, la), (b, lb)], o, l)


def final_kernel(group, *refs):
    *ins, o = refs
    blend(group, [(ins[i], ins[i + 1]) for i in range(0, len(ins), 2)], o)


def per_device(cores, queries, new_keys, new_values, cache_keys, cache_values, cache_len):
    tokens, heads, hd = queries.shape
    slots, kv, _ = cache_keys.shape
    n = lax.axis_size("ctx")
    chips = n // cores
    place = lax.axis_index("ctx")
    filled = jnp.clip(cache_len[0] - place * slots, 0, slots)
    chip, core = place // cores, place % cores

    def info(owner):
        return (owner - place) * tokens

    def over_core(x):
        return lax.ppermute(x, "ctx", [(i, i ^ 1) for i in range(n)])

    def over_chip(x, step):
        return lax.ppermute(
            x, "ctx", [(i, (i // cores + step) % chips * cores + i % cores) for i in range(n)]
        )

    part = jax.ShapeDtypeStruct(queries.shape, BF16)
    lse = jax.ShapeDtypeStruct((tokens * heads // 128, 128), F32)
    span = slots + tokens
    flops = 4 * tokens * heads * span * hd
    cost = lambda k: pl.CostEstimate(flops=k * flops, bytes_accessed=2 * 2**20, transcendentals=k * tokens * heads * span)
    q_chip = [over_chip(queries, step) for step in range(1, chips)]
    q_core = over_core(queries)
    q_diag = [over_core(q) for q in q_chip]
    sibling = place ^ 1
    own_n, own_l, sib_n, sib_l, keys, values = pl.pallas_call(
        first_kernel,
        out_shape=(
            part, lse, part, lse,
            jax.ShapeDtypeStruct((kv, span, hd), BF16),
            jax.ShapeDtypeStruct((kv, span, 2 * hd), BF16),
        ),
        in_specs=[SMEM] + [VMEM] * 6,
        out_specs=[VMEM] * 6,
        compiler_params=params(),
        cost_estimate=cost(2),
        name="own_and_sibling",
    )(jnp.stack([filled, info(place), info(sibling)]), queries, q_core, cache_keys, cache_values, new_keys, new_values)
    got = [own_n, own_l, over_core(sib_n), over_core(sib_l)]

    def attend_one(q, owner):
        return pl.pallas_call(
            next_kernel,
            out_shape=(part, lse),
            in_specs=[SMEM] + [VMEM] * 3,
            out_specs=[VMEM] * 2,
            compiler_params=params(),
            cost_estimate=cost(1),
            name="other_chip",
        )(jnp.stack([filled, info(owner)]), q, keys, values)

    for step in range(1, chips):
        from_chip = (chip - step) % chips
        d_n, d_l = attend_one(q_diag[step - 1], from_chip * cores + (1 - core))
        r_n, r_l = over_core(d_n), over_core(d_l)
        x_n, x_l = attend_one(q_chip[step - 1], from_chip * cores + core)
        c_n, c_l = pl.pallas_call(
            functools.partial(blend2_kernel, heads // kv),
            out_shape=(part, lse),
            in_specs=[VMEM] * 4,
            out_specs=[VMEM] * 2,
            compiler_params=params(),
            cost_estimate=pl.CostEstimate(flops=2**20, bytes_accessed=2**20, transcendentals=2**14),
            name="chip_sum",
        )(x_n, x_l, r_n, r_l)
        got += [over_chip(c_n, chips - step), over_chip(c_l, chips - step)]
    return pl.pallas_call(
        functools.partial(final_kernel, heads // kv),
        out_shape=part,
        in_specs=[VMEM] * len(got),
        out_specs=VMEM,
        compiler_params=params(),
        cost_estimate=pl.CostEstimate(flops=2**20, bytes_accessed=2**20, transcendentals=2**14),
        name="final_sum",
    )(*got)


def solution(mesh):
    spec = P(("conv", "ctx"), "head", None)
    return jax.shard_map(
        functools.partial(per_device, 2),
        mesh=mesh,
        in_specs=(spec,) * 5 + (P("conv"),),
        out_specs=spec,
        check_vma=False,
    )
```

```python
import functools
import math

import jax
import jax.numpy as jnp
from jax import lax
from jax.experimental import pallas as pl
from jax.experimental.pallas import tpu as pltpu
from jax.sharding import PartitionSpec as P

NEG_FILL = -1e30
LOG2E = 1.4426950408889634
VMEM = pl.BlockSpec(memory_space=pltpu.VMEM)
SMEM = pl.BlockSpec(memory_space=pltpu.SMEM)
HBM = pl.BlockSpec(memory_space=pltpu.HBM)
F32 = jnp.float32
BF16 = jnp.bfloat16
NT = (((1,), (1,)), ((), ()))
CORES = 2


def params():
    return pltpu.CompilerParams(vmem_limit_bytes=36 * 2**20)


def pack_rows(wide):
    eye = lax.broadcasted_iota(jnp.int32, (128, 128), 0) == lax.broadcasted_iota(jnp.int32, (128, 128), 1)
    return jnp.concatenate(
        [
            jnp.sum(jnp.where(eye, wide[i * 128 : (i + 1) * 128], 0.0), axis=0, keepdims=True)
            for i in range(wide.shape[0] // 128)
        ],
        axis=0,
    )


def spread_rows(packed):
    return jnp.concatenate(
        [jnp.transpose(jnp.broadcast_to(packed[i : i + 1, :], (128, 128))) for i in range(packed.shape[0])], axis=0
    )


def place_keys(filled, raw, new, keys):
    slots, kv, hd = raw.shape
    fresh = jnp.swapaxes(new[...], 0, 1)
    keys[:, slots:] = fresh

    @pl.when(filled == slots)
    def _():
        keys[:, 0:slots] = jnp.swapaxes(raw[...], 0, 1)

    @pl.when(filled < slots)
    def _():
        rows = jnp.swapaxes(raw[...], 0, 1)
        included = lax.broadcasted_iota(jnp.int32, (slots, hd), 0) < filled
        for h in range(kv):
            fill = jnp.where(filled > 0, rows[h, 0:1, :].astype(F32), fresh[h, 0:1, :].astype(F32))
            keys[h, 0:slots] = jnp.where(included, rows[h].astype(F32), fill).astype(BF16)


def place_values(filled, raw, new, values):
    slots, kv, hd = raw.shape
    fresh = new.shape[0]
    values[:, slots:, 0:hd] = jnp.swapaxes(new[...], 0, 1)
    values[:, slots:, hd:] = jnp.ones((kv, fresh, hd), BF16)

    @pl.when(filled == slots)
    def _():
        values[:, 0:slots, 0:hd] = jnp.swapaxes(raw[...], 0, 1)
        values[:, 0:slots, hd:] = jnp.ones((kv, slots, hd), BF16)

    @pl.when(filled < slots)
    def _():
        rows = jnp.swapaxes(raw[...], 0, 1)
        included = lax.broadcasted_iota(jnp.int32, (slots, hd), 0) < filled
        for h in range(kv):
            values[h, 0:slots, 0:hd] = jnp.where(included, rows[h].astype(F32), 0.0).astype(BF16)
            values[h, 0:slots, hd:] = jnp.where(included, 1.0, 0.0).astype(BF16)


def put_lse(ref, first, lse):
    heads = ref.shape[1]
    high = lse.astype(BF16).astype(F32)
    middle = (lse - high).astype(BF16).astype(F32)
    low = lse - high - middle
    extra = ref.shape[0] - first
    rest = jnp.zeros((extra * heads - 3 * lse.shape[0], 128), F32)
    rows = jnp.concatenate([high, middle, low, rest], axis=0)
    ref[first:] = rows.astype(BF16).reshape(extra, heads, 128)


def get_lse(ref, first):
    heads = ref.shape[1]
    n = first * heads // 128
    rows = ref[first:].astype(F32).reshape((ref.shape[0] - first) * heads, 128)
    return rows[0:n] + rows[n : 2 * n] + rows[2 * n : 3 * n]


def packed_shape(tokens, heads, hd):
    extra = -(-3 * (tokens * heads // 128) // heads)
    return jax.ShapeDtypeStruct((tokens + extra, heads, hd), BF16)


def attend(offset, fresh, q_ref, keys, values, parts, before_values=None):
    heads, hd = q_ref.shape[1:]
    kv, span, _ = keys.shape
    group = heads // kv
    slots = span - fresh
    scale = LOG2E / math.sqrt(hd)
    work = [(first, n, h, o) for first, n, o in parts for h in range(kv)]

    def scores(item):
        first, n, h, _ = item
        q = q_ref[first : first + n, h * group : (h + 1) * group, :].reshape(n * group, hd)
        s = lax.dot_general(q, keys[h, 0:slots], NT, preferred_element_type=F32)
        s2 = lax.dot_general(q, keys[h, slots:], NT, preferred_element_type=F32)
        return s, s2

    s, s2 = scores(work[0])
    if before_values is not None:
        before_values()
    lses = []
    for i, (first, n, h, o_ref) in enumerate(work):
        later = scores(work[i + 1]) if i + 1 < len(work) else (None, None)
        rows = n * group
        token = first + lax.broadcasted_iota(jnp.int32, (rows, fresh), 0) // group
        seen = token + offset >= lax.broadcasted_iota(jnp.int32, (rows, fresh), 1)
        s2 = jnp.where(seen, s2, NEG_FILL)
        peak = jnp.maximum(jnp.max(s, axis=-1, keepdims=True), jnp.max(s2, axis=-1, keepdims=True))
        w = jnp.exp2((s - peak) * scale).astype(BF16)
        w2 = jnp.where(seen, jnp.exp2((s2 - peak) * scale), 0.0).astype(BF16)
        out = jnp.dot(w, values[h, 0:slots], preferred_element_type=F32)
        out = out + jnp.dot(w2, values[h, slots:], preferred_element_type=F32)
        total = out[:, hd:]
        floored = jnp.maximum(total, 1.0)
        o_ref[0:n, h * group : (h + 1) * group, :] = (out[:, 0:hd] / floored).astype(BF16).reshape(n, group, hd)
        lses.append(pack_rows(jnp.where(total > 0.0, peak * (1.0 / math.sqrt(hd)) + jnp.log(floored), NEG_FILL)))
        if h == kv - 1:
            put_lse(o_ref, n, jnp.concatenate(lses, axis=0))
            lses = []
        s, s2 = later


def blend(parts, group):
    tokens, heads, hd = parts[0][0].shape
    top = functools.reduce(jnp.maximum, [lse for _, lse in parts])
    scales = [jnp.exp(lse - top) for _, lse in parts]
    total = functools.reduce(jnp.add, scales)
    lse = jnp.where(top > 0.5 * NEG_FILL, top + jnp.log(total), NEG_FILL)
    inv = 1.0 / total
    n = tokens * group // 128
    outs = []
    for h in range(heads // group):
        acc = None
        for (norm, _), s in zip(parts, scales):
            wide = spread_rows((s * inv)[h * n : (h + 1) * n, :])
            term = norm[:, h * group : (h + 1) * group, :].reshape(tokens * group, hd).astype(F32) * wide
            acc = term if acc is None else acc + term
        outs.append(acc)
    return outs, lse


def own_kernel(length, q, k, v, nk, nv, o, keys, values, q_in, k_in, v_in, nk_in, nv_in, sems):
    copies = [
        pltpu.make_async_copy(src, dst, sems.at[i])
        for i, (src, dst) in enumerate([(k, k_in), (nk, nk_in), (q, q_in), (v, v_in), (nv, nv_in)])
    ]
    for c in copies:
        c.start()
    slots = k.shape[0]
    filled = jnp.clip(length[0] - lax.axis_index("ctx") * slots, 0, slots)
    for c in copies[0:3]:
        c.wait()
    place_keys(filled, k_in, nk_in, keys)

    def fetch_values():
        for c in copies[3:]:
            c.wait()
        place_values(filled, v_in, nv_in, values)

    attend(0, nk.shape[0], q_in, keys, values, [(0, q.shape[0], o)], fetch_values)


def other_kernel(owner, first, n, q, keys, values, o):
    place = lax.axis_index("ctx")
    tokens = q.shape[0]
    attend((owner(place) - place) * tokens, tokens, q, keys, values, [(first, n, o)])


def chip_sum_kernel(group, first, n, tokens, a, b, o):
    heads, hd = a.shape[1:]
    lse_b = cut_lse(get_lse(b, tokens), heads // group, first, n, tokens)
    outs, lse = blend([(a[0:n], get_lse(a, n)), (b[first : first + n], lse_b)], group)
    for h, x in enumerate(outs):
        o[0:n, h * group : (h + 1) * group, :] = x.astype(BF16).reshape(n, group, hd)
    put_lse(o, n, lse)


def cut_lse(lse, kv, first, n, tokens):
    per = lse.shape[0] // kv
    a, b = first * per // tokens, (first + n) * per // tokens
    return jnp.concatenate([lse[h * per + a : h * per + b] for h in range(kv)], axis=0)


def near_kernel(group, own, sib, o, l):
    tokens, heads, hd = o.shape
    outs, lse = blend([(x[0:tokens], get_lse(x, tokens)) for x in (own, sib)], group)
    for h, x in enumerate(outs):
        o[:, h * group : (h + 1) * group, :] = x.reshape(tokens, group, hd)
    l[...] = lse


def final_kernel(group, halves, near, near_l, *refs):
    *far, o = refs
    tokens, heads, hd = o.shape
    n = tokens // halves
    for i in range(halves):
        first = i * n
        lse = cut_lse(near_l[...], heads // group, first, n, tokens)
        parts = [(near[first : first + n], lse)] + [(x[0:n], get_lse(x, n)) for x in far[i::halves]]
        outs, _ = blend(parts, group)
        for h, x in enumerate(outs):
            o[first : first + n, h * group : (h + 1) * group, :] = x.astype(BF16).reshape(n, group, hd)


def per_device(queries, new_keys, new_values, cache_keys, cache_values, cache_len):
    tokens, heads, hd = queries.shape
    slots, kv, _ = cache_keys.shape
    group = heads // kv
    n = lax.axis_size("ctx")
    chips = n // CORES
    halves = 2
    span = slots + tokens

    def over_core(x):
        return lax.ppermute(x, "ctx", [(i, i ^ 1) for i in range(n)])

    def over_chip(x, step):
        return lax.ppermute(x, "ctx", [(i, (i // CORES + step) % chips * CORES + i % CORES) for i in range(n)])

    def packed(m):
        return packed_shape(m, heads, hd)

    def cost(m):
        return pl.CostEstimate(
            flops=8 * m * heads * span * hd, bytes_accessed=4 * 2**20, transcendentals=m * heads * span
        )

    def call(name, kernel, out, args, estimate):
        return pl.pallas_call(
            kernel,
            out_shape=out,
            in_specs=[VMEM] * len(args),
            out_specs=jax.tree.map(lambda _: VMEM, out),
            compiler_params=params(),
            cost_estimate=estimate,
            name=name,
        )(*args)

    small = pl.CostEstimate(flops=2**20, bytes_accessed=2**20, transcendentals=2**14)
    q_chip = [over_chip(queries, step) for step in range(1, chips)]
    q_core = over_core(queries)
    pinned = [
        pltpu.with_memory_space_constraint(x, pltpu.HBM)
        for x in (queries, cache_keys, cache_values, new_keys, new_values)
    ]
    own, keys, values = pl.pallas_call(
        own_kernel,
        out_shape=[
            packed(tokens),
            jax.ShapeDtypeStruct((kv, span, hd), BF16),
            jax.ShapeDtypeStruct((kv, span, 2 * hd), BF16),
        ],
        in_specs=[SMEM] + [HBM] * 5,
        out_specs=[VMEM] * 3,
        scratch_shapes=[
            pltpu.VMEM(queries.shape, BF16),
            pltpu.VMEM(cache_keys.shape, BF16),
            pltpu.VMEM(cache_values.shape, BF16),
            pltpu.VMEM(new_keys.shape, BF16),
            pltpu.VMEM(new_values.shape, BF16),
            pltpu.SemaphoreType.DMA((5,)),
        ],
        compiler_params=params(),
        cost_estimate=cost(tokens),
        name="own",
    )(cache_len, *pinned)
    *q_chip, own = lax.optimization_barrier((*q_chip, own))
    q_diag = [over_core(q) for q in q_chip]

    def attend_other(name, q, owner, first, m):
        return call(name, functools.partial(other_kernel, owner, first, m), packed(m), (q, keys, values), cost(m))

    sib = over_core(attend_other("sibling", q_core, lambda i: i ^ 1, 0, tokens))
    m = tokens // halves
    far = []
    for step in range(1, chips):
        def same(i, step=step):
            return (i // CORES - step + chips) % chips * CORES + i % CORES

        diag = over_core(attend_other("diagonal", q_diag[step - 1], lambda i: same(i) ^ 1, 0, tokens))
        for i in range(halves):
            straight = attend_other("straight", q_chip[step - 1], same, i * m, m)
            both = call(
                "chip_sum", functools.partial(chip_sum_kernel, group, i * m, m, tokens), packed(m), (straight, diag), small
            )
            far.append(over_chip(both, chips - step))
    near = call(
        "near",
        functools.partial(near_kernel, group),
        [jax.ShapeDtypeStruct(queries.shape, F32), jax.ShapeDtypeStruct((tokens * heads // 128, 128), F32)],
        (own, sib),
        small,
    )
    return call(
        "final",
        functools.partial(final_kernel, group, halves),
        jax.ShapeDtypeStruct(queries.shape, BF16),
        (*near, *far),
        small,
    )


def solution(mesh):
    spec = P(("conv", "ctx"), "head", None)
    return jax.shard_map(
        per_device,
        mesh=mesh,
        in_specs=(spec,) * 5 + (P("conv"),),
        out_specs=spec,
        check_vma=False,
    )
```

```python
import functools
import math

import jax
import jax.numpy as jnp
from jax import lax
from jax.experimental import pallas as pl
from jax.experimental.pallas import tpu as pltpu
from jax.sharding import PartitionSpec as P

NEG_FILL = -1e30
LOG2E = 1.4426950408889634
VMEM = pl.BlockSpec(memory_space=pltpu.VMEM)
SMEM = pl.BlockSpec(memory_space=pltpu.SMEM)
HBM = pl.BlockSpec(memory_space=pltpu.HBM)
F32 = jnp.float32
BF16 = jnp.bfloat16
NT = (((1,), (1,)), ((), ()))
CORES = 2


def params():
    return pltpu.CompilerParams(vmem_limit_bytes=36 * 2**20)


def pack_rows(wide):
    eye = lax.broadcasted_iota(jnp.int32, (128, 128), 0) == lax.broadcasted_iota(jnp.int32, (128, 128), 1)
    return jnp.concatenate(
        [
            jnp.sum(jnp.where(eye, wide[i * 128 : (i + 1) * 128], 0.0), axis=0, keepdims=True)
            for i in range(wide.shape[0] // 128)
        ],
        axis=0,
    )


def spread_rows(packed):
    return jnp.concatenate(
        [jnp.transpose(jnp.broadcast_to(packed[i : i + 1, :], (128, 128))) for i in range(packed.shape[0])], axis=0
    )


def load_kernel(length, *refs):
    n = (len(refs) - 2) // 2
    ins, outs, filled, sems = refs[:n], refs[n : 2 * n], refs[-2], refs[-1]
    copies = [pltpu.make_async_copy(ins[i], outs[i], sems.at[i]) for i in range(n)]
    for c in copies:
        c.start()
    slots = ins[0].shape[0]
    filled[...] = jnp.full(filled.shape, jnp.clip(length[0] - lax.axis_index("ctx") * slots, 0, slots), jnp.int32)
    for c in copies:
        c.wait()


def prepare_kernel(filled, k, v, nk, keys, values):
    slots, kv, hd = k.shape
    count = filled[0:1, :]
    included = lax.broadcasted_iota(jnp.int32, (slots, hd), 0) < count
    k_rows, v_rows, nk_rows = [jnp.swapaxes(x[...], 0, 1) for x in (k, v, nk)]
    for h in range(kv):
        fill = jnp.where(count > 0, k_rows[h, 0:1].astype(F32), nk_rows[h, 0:1].astype(F32))
        keys[h] = jnp.where(included, k_rows[h].astype(F32), fill).astype(BF16)
        values[h, :, 0:hd] = jnp.where(included, v_rows[h].astype(F32), 0.0).astype(BF16)
        values[h, :, hd:] = jnp.where(included, 1.0, 0.0).astype(BF16)


def put_lse(ref, first, lse):
    heads = ref.shape[1]
    high = lse.astype(BF16).astype(F32)
    middle = (lse - high).astype(BF16).astype(F32)
    low = lse - high - middle
    extra = lse_rows(lse.shape[0], heads)
    rest = jnp.zeros((extra * heads - 3 * lse.shape[0], 128), F32)
    rows = jnp.concatenate([high, middle, low, rest], axis=0)
    ref[first : first + extra] = rows.astype(BF16).reshape(extra, heads, 128)


def lse_rows(n, heads):
    return -(-3 * n // heads)


def get_lse(ref, first):
    heads = ref.shape[1]
    n = first * heads // 128
    extra = lse_rows(n, heads)
    rows = ref[first : first + extra].astype(F32).reshape(extra * heads, 128)
    return rows[0:n] + rows[n : 2 * n] + rows[2 * n : 3 * n]


def packed_shape(tokens, heads, hd):
    return jax.ShapeDtypeStruct((tokens + lse_rows(tokens * heads // 128, heads), heads, hd), BF16)


def extended(shape, rows):
    return jax.ShapeDtypeStruct((shape.shape[0] + rows,) + shape.shape[1:], shape.dtype)


def attend(q_ref, keys, values, first, n, o_ref, fresh=None, causal=None):
    heads, hd = q_ref.shape[1:]
    kv = keys.shape[0]
    group = heads // kv
    rows = n * group
    scale = LOG2E / math.sqrt(hd)
    if causal is not None:
        count = fresh[0].shape[1]
        token = causal + lax.broadcasted_iota(jnp.int32, (rows, count), 0) // group
        seen = token >= lax.broadcasted_iota(jnp.int32, (rows, count), 1)

    def scores(h):
        q = q_ref[first : first + n, h * group : (h + 1) * group, :].reshape(rows, hd)
        found = [lax.dot_general(q, keys[h], NT, preferred_element_type=F32)]
        if fresh is not None:
            s = lax.dot_general(q, fresh[0][h], NT, preferred_element_type=F32)
            found.append(s if causal is None else jnp.where(seen, s, NEG_FILL))
        return found

    now = scores(0)
    lses = []
    for h in range(kv):
        later = scores(h + 1) if h + 1 < kv else None
        peak = functools.reduce(jnp.maximum, [jnp.max(s, axis=-1, keepdims=True) for s in now])
        weights = [jnp.exp2((s - peak) * scale) for s in now]
        if causal is not None:
            weights[1] = jnp.where(seen, weights[1], 0.0)
        out = jnp.dot(weights[0].astype(BF16), values[h], preferred_element_type=F32)
        if fresh is not None:
            out = out + jnp.dot(weights[1].astype(BF16), fresh[1][h], preferred_element_type=F32)
        total = out[:, hd:]
        floored = jnp.maximum(total, 1.0)
        o_ref[0:n, h * group : (h + 1) * group, :] = (out[:, 0:hd] / floored).astype(BF16).reshape(n, group, hd)
        lses.append(pack_rows(jnp.where(total > 0.0, peak * (1.0 / math.sqrt(hd)) + jnp.log(floored), NEG_FILL)))
        now = later
    put_lse(o_ref, n, jnp.concatenate(lses, axis=0))


def fresh_kernel(nk, nv, nk_core, nv_core, keys, values):
    low = lax.axis_index("ctx") % CORES == 0
    tokens, kv, hd = nk.shape
    for mine, other, out in ((nk, nk_core, keys), (nv, nv_core, values)):
        mine, other = [jnp.swapaxes(x[...], 0, 1).astype(F32) for x in (mine, other)]
        out[:, 0:tokens, 0:hd] = jnp.where(low, mine, other).astype(BF16)
        out[:, tokens:, 0:hd] = jnp.where(low, other, mine).astype(BF16)
    values[:, :, hd:] = jnp.ones((kv, CORES * tokens, hd), BF16)


def blend(parts, group):
    tokens, heads, hd = parts[0][0].shape
    top = functools.reduce(jnp.maximum, [lse for _, lse in parts])
    scales = [jnp.exp(lse - top) for _, lse in parts]
    total = functools.reduce(jnp.add, scales)
    lse = jnp.where(top > 0.5 * NEG_FILL, top + jnp.log(total), NEG_FILL)
    inv = 1.0 / total
    n = tokens * group // 128
    outs = []
    for h in range(heads // group):
        norms = [
            norm[:, h * group : (h + 1) * group, :].reshape(tokens * group, hd).astype(F32) for norm, _ in parts
        ]
        acc = norms[0]
        for norm, s in zip(norms[1:], scales[1:]):
            acc = acc + (norm - norms[0]) * spread_rows((s * inv)[h * n : (h + 1) * n, :])
        outs.append(acc)
    return outs, lse


def shard_kernel(first, n, q, keys, values, *refs):
    o = refs[-1]
    attend(q, keys, values, first, n, o)
    if len(refs) > 1:
        o[o.shape[0] - refs[0].shape[0] :] = refs[0][...]


def straight_kernel(owner, first, n, q, keys, values, fresh_k, fresh_v, o):
    place = lax.axis_index("ctx")
    sees = owner(place) > place

    @pl.when(sees)
    def _():
        attend(q, keys, values, first, n, o, (fresh_k, fresh_v))

    @pl.when(jnp.logical_not(sees))
    def _():
        attend(q, keys, values, first, n, o)


def own_kernel(q, keys, values, fresh_k, fresh_v, o):
    tokens = q.shape[0]
    core = lax.axis_index("ctx") % CORES
    attend(q, keys, values, 0, tokens, o, (fresh_k, fresh_v), core * tokens)


def chip_sum_kernel(group, n, a, b, o):
    heads, hd = o.shape[1:]
    outs, lse = blend([(x[0:n], get_lse(x, n)) for x in (a, b)], group)
    for h, x in enumerate(outs):
        o[0:n, h * group : (h + 1) * group, :] = x.astype(BF16).reshape(n, group, hd)
    put_lse(o, n, lse)
    used = packed_shape(n, heads, hd).shape[0]
    if o.shape[0] > used:
        o[used:] = jnp.zeros((o.shape[0] - used, heads, hd), BF16)


def cut_lse(lse, kv, first, n, tokens):
    per = lse.shape[0] // kv
    a, b = first * per // tokens, (first + n) * per // tokens
    return jnp.concatenate([lse[h * per + a : h * per + b] for h in range(kv)], axis=0)


def near_kernel(group, own, sib, o, l):
    tokens, heads, hd = o.shape
    sib = sib.at[pl.ds(sib.shape[0] - own.shape[0], own.shape[0])]
    outs, lse = blend([(x[0:tokens], get_lse(x, tokens)) for x in (own, sib)], group)
    for h, x in enumerate(outs):
        o[:, h * group : (h + 1) * group, :] = x.reshape(tokens, group, hd)
    l[...] = lse


def final_kernel(group, shares, near, near_l, *refs):
    *far, o = refs
    tokens, heads, hd = o.shape
    for i, (first, n) in enumerate(shares):
        lse = cut_lse(near_l[...], heads // group, first, n, tokens)
        parts = [(near[first : first + n], lse)] + [(x[0:n], get_lse(x, n)) for x in far[i :: len(shares)]]
        outs, _ = blend(parts, group)
        for h, x in enumerate(outs):
            o[first : first + n, h * group : (h + 1) * group, :] = x.astype(BF16).reshape(n, group, hd)


def per_device(queries, new_keys, new_values, cache_keys, cache_values, cache_len):
    tokens, heads, hd = queries.shape
    slots, kv, _ = cache_keys.shape
    group = heads // kv
    n = lax.axis_size("ctx")
    chips = n // CORES
    unit = max(1, 128 // group)
    late = max(unit, tokens // 2 // unit * unit)
    shares = [(0, tokens - late), (tokens - late, late)]

    def over_core(x):
        return lax.ppermute(x, "ctx", [(i, i ^ 1) for i in range(n)])

    def over_chip(x, step):
        return lax.ppermute(x, "ctx", [(i, (i // CORES + step) % chips * CORES + i % CORES) for i in range(n)])

    def packed(m):
        return packed_shape(m, heads, hd)

    def cost(m):
        return pl.CostEstimate(
            flops=8 * m * heads * slots * hd, bytes_accessed=4 * 2**20, transcendentals=m * heads * slots
        )

    def call(name, kernel, out, args, estimate):
        return pl.pallas_call(
            kernel,
            out_shape=out,
            in_specs=[VMEM] * len(args),
            out_specs=jax.tree.map(lambda _: VMEM, out),
            compiler_params=params(),
            cost_estimate=estimate,
            name=name,
        )(*args)

    tiny = pl.CostEstimate(flops=0, bytes_accessed=0, transcendentals=0)
    small = pl.CostEstimate(flops=2**20, bytes_accessed=2**20, transcendentals=2**14)
    q_chip = [over_chip(queries, step) for step in range(1, chips)]
    moved = (cache_keys, cache_values, new_keys, new_values, queries)
    k, v, nk, nv, q_own, filled = pl.pallas_call(
        load_kernel,
        out_shape=[jax.ShapeDtypeStruct(x.shape, x.dtype) for x in moved]
        + [jax.ShapeDtypeStruct((8, hd), jnp.int32)],
        in_specs=[SMEM] + [HBM] * len(moved),
        out_specs=[VMEM] * (len(moved) + 1),
        scratch_shapes=[pltpu.SemaphoreType.DMA((len(moved),))],
        compiler_params=params(),
        cost_estimate=small,
        name="load",
    )(cache_len, *[pltpu.with_memory_space_constraint(x, pltpu.HBM) for x in moved])
    q_core, nk_core, nv_core = over_core(queries), over_core(new_keys), over_core(new_values)
    q_core, nk_core, nv_core = lax.optimization_barrier((q_core, nk_core, nv_core))
    keys, values = call(
        "prepare",
        prepare_kernel,
        [jax.ShapeDtypeStruct((kv, slots, hd), BF16), jax.ShapeDtypeStruct((kv, slots, 2 * hd), BF16)],
        (filled, k, v, nk),
        small,
    )
    shard = (keys, values)
    fresh = call(
        "fresh",
        fresh_kernel,
        [jax.ShapeDtypeStruct((kv, CORES * tokens, hd), BF16), jax.ShapeDtypeStruct((kv, CORES * tokens, 2 * hd), BF16)],
        (nk, nv, nk_core, nv_core),
        small,
    )
    q_core, *fresh = lax.optimization_barrier((q_core, *fresh))

    def attend_part(name, kernel, m, *args):
        return call(name, kernel, packed(m), args, cost(m))

    sib = attend_part("sibling", functools.partial(shard_kernel, 0, tokens), tokens, q_core, *shard)
    *q_chip, sib = lax.optimization_barrier((*q_chip, sib))
    q_diag = [over_core(q) for q in q_chip]
    far = []
    for step in range(1, chips):
        def owner(i, step=step):
            return (i // CORES - step + chips) % chips * CORES + i % CORES

        def straight_part(q, first, m):
            kernel = functools.partial(straight_kernel, owner, first, m)
            return call("straight", kernel, packed(m), (q, *shard, *fresh), tiny if first else cost(m))

        q_s, q_d = q_chip[step - 1], q_diag[step - 1]
        early = straight_part(q_s, *shares[0])
        q_d, early = lax.optimization_barrier((q_d, early))
        diag = []
        for first, m in shares:
            more = [sib] if first == 0 and step == 1 else []
            kernel = functools.partial(shard_kernel, first, m)
            shape = extended(packed(m), sum(x.shape[0] for x in more))
            diag.append(call("diagonal", kernel, shape, (q_d, *shard, *more), cost(m)))
            q_d, diag[-1] = lax.optimization_barrier((q_d, diag[-1]))
        q_s, diag[-1] = lax.optimization_barrier((q_s, diag[-1]))
        diag = [over_core(x) for x in diag]
        if step == 1:
            from_sib = diag[0]
        for i, (first, m) in enumerate(shares):
            straight = straight_part(q_s, first, m) if i else early
            shape = extended(packed(m), len(shares) - 1 - i)
            both = call("chip_sum", functools.partial(chip_sum_kernel, group, m), shape, (diag[i], straight), tiny)
            q_s, q_own, both = lax.optimization_barrier((q_s, q_own, both))
            far.append(over_chip(both, chips - step))
    own = call("own", own_kernel, packed(tokens), (q_own, *shard, *fresh), tiny)
    near = call(
        "near",
        functools.partial(near_kernel, group),
        [jax.ShapeDtypeStruct(queries.shape, F32), jax.ShapeDtypeStruct((tokens * heads // 128, 128), F32)],
        (own, from_sib),
        tiny,
    )
    return call(
        "final",
        functools.partial(final_kernel, group, shares),
        jax.ShapeDtypeStruct(queries.shape, BF16),
        (*near, *far),
        small,
    )


def solution(mesh):
    spec = P(("conv", "ctx"), "head", None)
    return jax.shard_map(
        per_device,
        mesh=mesh,
        in_specs=(spec,) * 5 + (P("conv"),),
        out_specs=spec,
        check_vma=False,
    )
```

```python
import functools
import math

import jax
import jax.numpy as jnp
from jax import lax
from jax.experimental import pallas as pl
from jax.experimental.pallas import tpu as pltpu
from jax.sharding import PartitionSpec as P

NEG_FILL = -1e30
LOG2E = 1.4426950408889634
VMEM = pl.BlockSpec(memory_space=pltpu.VMEM)
SMEM = pl.BlockSpec(memory_space=pltpu.SMEM)
HBM = pl.BlockSpec(memory_space=pltpu.HBM)
F32 = jnp.float32
BF16 = jnp.bfloat16
NT = (((1,), (1,)), ((), ()))
CORES = 2


def params():
    return pltpu.CompilerParams(vmem_limit_bytes=36 * 2**20)


def pack_rows(wide):
    eye = lax.broadcasted_iota(jnp.int32, (128, 128), 0) == lax.broadcasted_iota(jnp.int32, (128, 128), 1)
    return jnp.concatenate(
        [
            jnp.sum(jnp.where(eye, wide[i * 128 : (i + 1) * 128], 0.0), axis=0, keepdims=True)
            for i in range(wide.shape[0] // 128)
        ],
        axis=0,
    )


def spread_rows(packed):
    return jnp.concatenate(
        [jnp.transpose(jnp.broadcast_to(packed[i : i + 1, :], (128, 128))) for i in range(packed.shape[0])], axis=0
    )


def load_kernel(pieces, *refs):
    *refs, held, sems = refs
    n = (len(refs) - 1 - pieces) // 2
    length, ins, outs, filled = refs[0], refs[1 : n + 1], refs[n + 1 : -1], refs[-1]
    moves = list(zip(ins[:-1], outs))
    for i in range(pieces):
        m = outs[-1].shape[0]
        moves.append((ins[-1].at[i * m : (i + 1) * m], outs[len(ins) - 1 + i]))
    moves.append((length, held))
    copies = [pltpu.make_async_copy(a, b, sems.at[i]) for i, (a, b) in enumerate(moves)]
    for c in copies[::-1]:
        c.start()
    slots = ins[0].shape[0]
    copies[-1].wait()
    filled[...] = jnp.full(filled.shape, jnp.clip(held[0] - lax.axis_index("ctx") * slots, 0, slots), jnp.int32)
    for c in copies[:-1]:
        c.wait()


def prepare_kernel(filled, k, v, nk, keys, values):
    slots, kv, hd = k.shape
    count = filled[0:1, :]
    included = lax.broadcasted_iota(jnp.int32, (slots, hd), 0) < count
    k_rows, v_rows, nk_rows = [jnp.swapaxes(x[...], 0, 1) for x in (k, v, nk)]
    for h in range(kv):
        fill = jnp.where(count > 0, k_rows[h, 0:1].astype(F32), nk_rows[h, 0:1].astype(F32))
        keys[h] = jnp.where(included, k_rows[h].astype(F32), fill).astype(BF16)
        values[h, :, 0:hd] = jnp.where(included, v_rows[h].astype(F32), 0.0).astype(BF16)
        values[h, :, hd:] = jnp.where(included, 1.0, 0.0).astype(BF16)


def put_lse(ref, first, lse):
    heads = ref.shape[1]
    high = lse.astype(BF16).astype(F32)
    middle = (lse - high).astype(BF16).astype(F32)
    low = lse - high - middle
    extra = lse_rows(lse.shape[0], heads)
    rest = jnp.zeros((extra * heads - 3 * lse.shape[0], 128), F32)
    rows = jnp.concatenate([high, middle, low, rest], axis=0)
    ref[first : first + extra] = rows.astype(BF16).reshape(extra, heads, 128)


def lse_rows(n, heads):
    return -(-3 * n // heads)


def get_lse(ref, first):
    heads = ref.shape[1]
    n = first * heads // 128
    extra = lse_rows(n, heads)
    rows = ref[first : first + extra].astype(F32).reshape(extra * heads, 128)
    return rows[0:n] + rows[n : 2 * n] + rows[2 * n : 3 * n]


def packed_shape(tokens, heads, hd):
    return jax.ShapeDtypeStruct((tokens + lse_rows(tokens * heads // 128, heads), heads, hd), BF16)


def extended(shape, rows):
    return jax.ShapeDtypeStruct((shape.shape[0] + rows,) + shape.shape[1:], shape.dtype)


def attend(q_refs, keys, values, first, n, o_ref, fresh=None, causal=None):
    heads, hd = q_refs[0].shape[1:]
    kv = keys.shape[0]
    group = heads // kv
    rows = n * group
    scale = LOG2E / math.sqrt(hd)
    if causal is not None:
        count = fresh[0].shape[1]
        token = causal + lax.broadcasted_iota(jnp.int32, (rows, count), 0) // group
        seen = token >= lax.broadcasted_iota(jnp.int32, (rows, count), 1)

    def scores(h):
        cut = slice(h * group, (h + 1) * group)
        if len(q_refs) == 1:
            q = q_refs[0][first : first + n, cut, :].reshape(rows, hd)
        else:
            q = jnp.concatenate([x[:, cut, :].reshape(x.shape[0] * group, hd) for x in q_refs], axis=0)
        found = [lax.dot_general(q, keys[h], NT, preferred_element_type=F32)]
        if fresh is not None:
            s = lax.dot_general(q, fresh[0][h], NT, preferred_element_type=F32)
            found.append(s if causal is None else jnp.where(seen, s, NEG_FILL))
        return found

    now = scores(0)
    lses = []
    for h in range(kv):
        later = scores(h + 1) if h + 1 < kv else None
        peak = functools.reduce(jnp.maximum, [jnp.max(s, axis=-1, keepdims=True) for s in now])
        weights = [jnp.exp2((s - peak) * scale) for s in now]
        if causal is not None:
            weights[1] = jnp.where(seen, weights[1], 0.0)
        out = jnp.dot(weights[0].astype(BF16), values[h], preferred_element_type=F32)
        if fresh is not None:
            out = out + jnp.dot(weights[1].astype(BF16), fresh[1][h], preferred_element_type=F32)
        total = out[:, hd:]
        floored = jnp.maximum(total, 1.0)
        o_ref[0:n, h * group : (h + 1) * group, :] = (out[:, 0:hd] / floored).astype(BF16).reshape(n, group, hd)
        lses.append(pack_rows(jnp.where(total > 0.0, peak * (1.0 / math.sqrt(hd)) + jnp.log(floored), NEG_FILL)))
        now = later
    put_lse(o_ref, n, jnp.concatenate(lses, axis=0))


def fresh_kernel(nk, nv, nk_core, nv_core, keys, values):
    low = lax.axis_index("ctx") % CORES == 0
    tokens, kv, hd = nk.shape
    for mine, other, out in ((nk, nk_core, keys), (nv, nv_core, values)):
        mine, other = [jnp.swapaxes(x[...], 0, 1).astype(F32) for x in (mine, other)]
        out[:, 0:tokens, 0:hd] = jnp.where(low, mine, other).astype(BF16)
        out[:, tokens:, 0:hd] = jnp.where(low, other, mine).astype(BF16)
    values[:, :, hd:] = jnp.ones((kv, CORES * tokens, hd), BF16)


def blend(parts, group):
    tokens, heads, hd = parts[0][0].shape
    top = functools.reduce(jnp.maximum, [lse for _, lse in parts])
    scales = [jnp.exp(lse - top) for _, lse in parts]
    total = functools.reduce(jnp.add, scales)
    lse = jnp.where(top > 0.5 * NEG_FILL, top + jnp.log(total), NEG_FILL)
    inv = 1.0 / total
    n = tokens * group // 128
    outs = []
    for h in range(heads // group):
        norms = [
            norm[:, h * group : (h + 1) * group, :].reshape(tokens * group, hd).astype(F32) for norm, _ in parts
        ]
        acc = norms[0]
        for norm, s in zip(norms[1:], scales[1:]):
            acc = acc + (norm - norms[0]) * spread_rows((s * inv)[h * n : (h + 1) * n, :])
        outs.append(acc)
    return outs, lse


def shard_kernel(first, n, q, keys, values, *refs):
    o = refs[-1]
    attend([q], keys, values, first, n, o)
    if len(refs) > 1:
        o[o.shape[0] - refs[0].shape[0] :] = refs[0][...]


def straight_kernel(owner, first, n, q, keys, values, fresh_k, fresh_v, o):
    place = lax.axis_index("ctx")
    sees = owner(place) > place

    @pl.when(sees)
    def _():
        attend([q], keys, values, first, n, o, (fresh_k, fresh_v))

    @pl.when(jnp.logical_not(sees))
    def _():
        attend([q], keys, values, first, n, o)


def sibling_kernel(*refs):
    *q, keys, values, o = refs
    attend(q, keys, values, 0, sum(x.shape[0] for x in q), o)


def own_kernel(*refs):
    *q, keys, values, fresh_k, fresh_v, o = refs
    tokens = sum(x.shape[0] for x in q)
    core = lax.axis_index("ctx") % CORES
    attend(q, keys, values, 0, tokens, o, (fresh_k, fresh_v), core * tokens)


def chip_sum_kernel(group, n, a, b, o):
    heads, hd = o.shape[1:]
    outs, lse = blend([(x[0:n], get_lse(x, n)) for x in (a, b)], group)
    for h, x in enumerate(outs):
        o[0:n, h * group : (h + 1) * group, :] = x.astype(BF16).reshape(n, group, hd)
    put_lse(o, n, lse)
    used = packed_shape(n, heads, hd).shape[0]
    if o.shape[0] > used:
        o[used:] = jnp.zeros((o.shape[0] - used, heads, hd), BF16)


def cut_lse(lse, kv, first, n, tokens):
    per = lse.shape[0] // kv
    a, b = first * per // tokens, (first + n) * per // tokens
    return jnp.concatenate([lse[h * per + a : h * per + b] for h in range(kv)], axis=0)


def near_kernel(group, own, sib, o, l):
    tokens, heads, hd = o.shape
    sib = sib.at[pl.ds(sib.shape[0] - own.shape[0], own.shape[0])]
    outs, lse = blend([(x[0:tokens], get_lse(x, tokens)) for x in (own, sib)], group)
    for h, x in enumerate(outs):
        o[:, h * group : (h + 1) * group, :] = x.reshape(tokens, group, hd)
    l[...] = lse


def final_kernel(group, shares, near, near_l, *refs):
    *far, o = refs
    tokens, heads, hd = o.shape
    for i, (first, n) in enumerate(shares):
        lse = cut_lse(near_l[...], heads // group, first, n, tokens)
        parts = [(near[first : first + n], lse)] + [(x[0:n], get_lse(x, n)) for x in far[i :: len(shares)]]
        outs, _ = blend(parts, group)
        for h, x in enumerate(outs):
            o[first : first + n, h * group : (h + 1) * group, :] = x.astype(BF16).reshape(n, group, hd)


def per_device(queries, new_keys, new_values, cache_keys, cache_values, cache_len):
    tokens, heads, hd = queries.shape
    slots, kv, _ = cache_keys.shape
    group = heads // kv
    n = lax.axis_size("ctx")
    chips = n // CORES
    unit = max(1, 128 // group)
    late = max(unit, tokens // 2 // unit * unit)
    shares = [(0, tokens - late), (tokens - late, late)]

    def over_core(x):
        return lax.ppermute(x, "ctx", [(i, i ^ 1) for i in range(n)])

    def over_chip(x, step):
        return lax.ppermute(x, "ctx", [(i, (i // CORES + step) % chips * CORES + i % CORES) for i in range(n)])

    def packed(m):
        return packed_shape(m, heads, hd)

    def cost(m):
        return pl.CostEstimate(
            flops=8 * m * heads * slots * hd, bytes_accessed=4 * 2**20, transcendentals=m * heads * slots
        )

    def call(name, kernel, out, args, estimate):
        return pl.pallas_call(
            kernel,
            out_shape=out,
            in_specs=[VMEM] * len(args),
            out_specs=jax.tree.map(lambda _: VMEM, out),
            compiler_params=params(),
            cost_estimate=estimate,
            name=name,
        )(*args)

    tiny = pl.CostEstimate(flops=0, bytes_accessed=0, transcendentals=0)
    small = pl.CostEstimate(flops=2**20, bytes_accessed=2**20, transcendentals=2**14)
    q_chip = [over_chip(queries, step) for step in range(1, chips)]
    moved = (cache_keys, cache_values, new_keys, new_values, queries)
    pieces = 2
    out = [jax.ShapeDtypeStruct(x.shape, x.dtype) for x in moved[:-1]]
    out += [jax.ShapeDtypeStruct((tokens // pieces, heads, hd), BF16)] * pieces
    out += [jax.ShapeDtypeStruct((8, hd), jnp.int32)]
    k, v, nk, nv, *q_own, filled = pl.pallas_call(
        functools.partial(load_kernel, pieces),
        out_shape=out,
        in_specs=[pl.BlockSpec(memory_space=pl.ANY)] + [HBM] * len(moved),
        out_specs=[VMEM] * len(out),
        scratch_shapes=[pltpu.SMEM((1,), jnp.int32), pltpu.SemaphoreType.DMA((len(out),))],
        compiler_params=params(),
        cost_estimate=tiny,
        name="load",
    )(cache_len, *[pltpu.with_memory_space_constraint(x, pltpu.HBM) for x in moved])
    q_core, nk_core, nv_core = [over_core(x) for x in q_own], over_core(nk), over_core(nv)
    *q_core, nk_core, nv_core = lax.optimization_barrier((*q_core, nk_core, nv_core))
    keys, values = call(
        "prepare",
        prepare_kernel,
        [jax.ShapeDtypeStruct((kv, slots, hd), BF16), jax.ShapeDtypeStruct((kv, slots, 2 * hd), BF16)],
        (filled, k, v, nk),
        tiny,
    )
    shard = (keys, values)
    fresh = call(
        "fresh",
        fresh_kernel,
        [jax.ShapeDtypeStruct((kv, CORES * tokens, hd), BF16), jax.ShapeDtypeStruct((kv, CORES * tokens, 2 * hd), BF16)],
        (nk, nv, nk_core, nv_core),
        tiny,
    )
    *q_core, fresh_k, fresh_v = lax.optimization_barrier((*q_core, *fresh))
    fresh = (fresh_k, fresh_v)

    def attend_part(name, kernel, m, *args):
        return call(name, kernel, packed(m), args, cost(m))

    sib = call("sibling", sibling_kernel, packed(tokens), (*q_core, *shard), tiny)
    *q_chip, sib = lax.optimization_barrier((*q_chip, sib))
    q_diag = [over_core(q) for q in q_chip]
    far = []
    for step in range(1, chips):
        def owner(i, step=step):
            return (i // CORES - step + chips) % chips * CORES + i % CORES

        def straight_part(q, first, m):
            kernel = functools.partial(straight_kernel, owner, first, m)
            return call("straight", kernel, packed(m), (q, *shard, *fresh), tiny if first else cost(m))

        q_s, q_d = q_chip[step - 1], q_diag[step - 1]
        early = straight_part(q_s, *shares[0])
        q_d, early = lax.optimization_barrier((q_d, early))
        diag = []
        for first, m in shares:
            more = [sib] if first == 0 and step == 1 else []
            kernel = functools.partial(shard_kernel, first, m)
            shape = extended(packed(m), sum(x.shape[0] for x in more))
            diag.append(call("diagonal", kernel, shape, (q_d, *shard, *more), cost(m)))
            q_d, diag[-1] = lax.optimization_barrier((q_d, diag[-1]))
        q_s, diag[-1] = lax.optimization_barrier((q_s, diag[-1]))
        diag = [over_core(x) for x in diag]
        if step == 1:
            from_sib = diag[0]
        for i, (first, m) in enumerate(shares):
            straight = straight_part(q_s, first, m) if i else early
            shape = extended(packed(m), len(shares) - 1 - i)
            both = call("chip_sum", functools.partial(chip_sum_kernel, group, m), shape, (diag[i], straight), tiny)
            q_s, both, *q_own = lax.optimization_barrier((q_s, both, *q_own))
            far.append(over_chip(both, chips - step))
    own = call("own", own_kernel, packed(tokens), (*q_own, *shard, *fresh), tiny)
    near = call(
        "near",
        functools.partial(near_kernel, group),
        [jax.ShapeDtypeStruct(queries.shape, F32), jax.ShapeDtypeStruct((tokens * heads // 128, 128), F32)],
        (own, from_sib),
        tiny,
    )
    return call(
        "final",
        functools.partial(final_kernel, group, shares),
        jax.ShapeDtypeStruct(queries.shape, BF16),
        (*near, *far),
        small,
    )


def solution(mesh):
    spec = P(("conv", "ctx"), "head", None)
    return jax.shard_map(
        per_device,
        mesh=mesh,
        in_specs=(spec,) * 5 + (P("conv"),),
        out_specs=spec,
        check_vma=False,
    )
```

```python
import functools
import math

import jax
import jax.numpy as jnp
from jax import lax
from jax.experimental import pallas as pl
from jax.experimental.pallas import tpu as pltpu
from jax.sharding import PartitionSpec as P

NEG_FILL = -1e30
LOG2E = 1.4426950408889634
VMEM = pl.BlockSpec(memory_space=pltpu.VMEM)
SMEM = pl.BlockSpec(memory_space=pltpu.SMEM)
HBM = pl.BlockSpec(memory_space=pltpu.HBM)
F32 = jnp.float32
BF16 = jnp.bfloat16
NT = (((1,), (1,)), ((), ()))
CORES = 2


def params():
    return pltpu.CompilerParams(vmem_limit_bytes=36 * 2**20)


def pack_rows(wide):
    eye = lax.broadcasted_iota(jnp.int32, (128, 128), 0) == lax.broadcasted_iota(jnp.int32, (128, 128), 1)
    return jnp.concatenate(
        [
            jnp.sum(jnp.where(eye, wide[i * 128 : (i + 1) * 128], 0.0), axis=0, keepdims=True)
            for i in range(wide.shape[0] // 128)
        ],
        axis=0,
    )


def spread_rows(packed):
    return jnp.concatenate(
        [jnp.transpose(jnp.broadcast_to(packed[i : i + 1, :], (128, 128))) for i in range(packed.shape[0])], axis=0
    )


def load_kernel(length, k, v, q, nk, nv, k_out, v_out, qk, qv, filled, held, sems):
    m = q.shape[0] // 2
    moves = [(k, k_out), (v, v_out)]
    for i, (new, out) in enumerate(((nk, qk), (nv, qv))):
        moves += [(q.at[i * m : (i + 1) * m], out.at[0:m]), (new, out.at[m:])]
    moves.append((length, held))
    copies = [pltpu.make_async_copy(a, b, sems.at[i]) for i, (a, b) in enumerate(moves)]
    for c in copies[::-1]:
        c.start()
    slots = k.shape[0]
    copies[-1].wait()
    filled[...] = jnp.full(filled.shape, jnp.clip(held[0] - lax.axis_index("ctx") * slots, 0, slots), jnp.int32)
    for c in copies[:-1]:
        c.wait()


def prepare_kernel(new, filled, k, v, qk, keys, values):
    slots, kv, hd = k.shape
    keys[...] = jnp.swapaxes(k[...], 0, 1)
    values[:, :, 0:hd] = jnp.swapaxes(v[...], 0, 1)
    values[:, :, hd:] = jnp.ones((kv, slots, hd), BF16)

    @pl.when(filled[0, 0] < slots)
    def _():
        count = filled[0:1, :]
        included = lax.broadcasted_iota(jnp.int32, (slots, hd), 0) < count
        first = qk[new].astype(F32)
        for h in range(kv):
            fill = jnp.where(count > 0, keys[h, 0:1, :].astype(F32), first[h : h + 1])
            keys[h] = jnp.where(included, keys[h].astype(F32), fill).astype(BF16)
            values[h, :, 0:hd] = jnp.where(included, values[h, :, 0:hd].astype(F32), 0.0).astype(BF16)
            values[h, :, hd:] = jnp.where(included, 1.0, 0.0).astype(BF16)


def put_lse(ref, first, lse):
    heads = ref.shape[1]
    high = lse.astype(BF16).astype(F32)
    middle = (lse - high).astype(BF16).astype(F32)
    low = lse - high - middle
    extra = lse_rows(lse.shape[0], heads)
    rest = jnp.zeros((extra * heads - 3 * lse.shape[0], 128), F32)
    rows = jnp.concatenate([high, middle, low, rest], axis=0)
    ref[first : first + extra] = rows.astype(BF16).reshape(extra, heads, 128)


def lse_rows(n, heads):
    return -(-3 * n // heads)


def get_lse(ref, first):
    heads = ref.shape[1]
    n = first * heads // 128
    extra = lse_rows(n, heads)
    rows = ref[first : first + extra].astype(F32).reshape(extra * heads, 128)
    return rows[0:n] + rows[n : 2 * n] + rows[2 * n : 3 * n]


def packed_shape(tokens, heads, hd):
    return jax.ShapeDtypeStruct((tokens + lse_rows(tokens * heads // 128, heads), heads, hd), BF16)


def extended(shape, rows):
    return jax.ShapeDtypeStruct((shape.shape[0] + rows,) + shape.shape[1:], shape.dtype)


def attend(q_refs, keys, values, first, n, o_ref, fresh=None, causal=None):
    heads, hd = q_refs[0].shape[1:]
    kv = keys.shape[0]
    group = heads // kv
    rows = n * group
    scale = LOG2E / math.sqrt(hd)
    if causal is not None:
        count = fresh[0].shape[1]
        token = causal + lax.broadcasted_iota(jnp.int32, (rows, count), 0) // group
        seen = token >= lax.broadcasted_iota(jnp.int32, (rows, count), 1)

    def scores(h):
        cut = slice(h * group, (h + 1) * group)
        if len(q_refs) == 1:
            q = q_refs[0][first : first + n, cut, :].reshape(rows, hd)
        else:
            m = n // len(q_refs)
            q = jnp.concatenate([x[0:m, cut, :].reshape(m * group, hd) for x in q_refs], axis=0)
        found = [lax.dot_general(q, keys[h], NT, preferred_element_type=F32)]
        if fresh is not None:
            s = lax.dot_general(q, fresh[0][h], NT, preferred_element_type=F32)
            found.append(s if causal is None else jnp.where(seen, s, NEG_FILL))
        return found

    now = scores(0)
    lses = []
    for h in range(kv):
        later = scores(h + 1) if h + 1 < kv else None
        peak = functools.reduce(jnp.maximum, [jnp.max(s, axis=-1, keepdims=True) for s in now])
        weights = [jnp.exp2((s - peak) * scale) for s in now]
        if causal is not None:
            weights[1] = jnp.where(seen, weights[1], 0.0)
        out = jnp.dot(weights[0].astype(BF16), values[h], preferred_element_type=F32)
        if fresh is not None:
            out = out + jnp.dot(weights[1].astype(BF16), fresh[1][h], preferred_element_type=F32)
        total = out[:, hd:]
        floored = jnp.maximum(total, 1.0)
        o_ref[0:n, h * group : (h + 1) * group, :] = (out[:, 0:hd] / floored).astype(BF16).reshape(n, group, hd)
        lses.append(pack_rows(jnp.where(total > 0.0, peak * (1.0 / math.sqrt(hd)) + jnp.log(floored), NEG_FILL)))
        now = later
    put_lse(o_ref, n, jnp.concatenate(lses, axis=0))


def fresh_kernel(m, qk, qv, qk_core, qv_core, keys, values, rows):
    low = lax.axis_index("ctx") % CORES == 0
    kv, count, hd = keys.shape
    tokens = count // CORES
    for mine, other, out in ((qk, qk_core, keys), (qv, qv_core, values)):
        mine, other = mine[m:].astype(F32), other[m:].astype(F32)
        for i, x in enumerate((jnp.where(low, mine, other), jnp.where(low, other, mine))):
            rows[...] = x.reshape(tokens * kv, hd)
            for h in range(kv):
                out[h, i * tokens : (i + 1) * tokens, 0:hd] = rows[pl.ds(h, tokens, stride=kv), :].astype(BF16)
    values[:, :, hd:] = jnp.ones((kv, count, hd), BF16)


def blend(parts, group):
    tokens, heads, hd = parts[0][0].shape
    top = functools.reduce(jnp.maximum, [lse for _, lse in parts])
    scales = [jnp.exp(lse - top) for _, lse in parts]
    total = functools.reduce(jnp.add, scales)
    lse = jnp.where(top > 0.5 * NEG_FILL, top + jnp.log(total), NEG_FILL)
    inv = 1.0 / total
    n = tokens * group // 128
    outs = []
    for h in range(heads // group):
        norms = [
            norm[:, h * group : (h + 1) * group, :].reshape(tokens * group, hd).astype(F32) for norm, _ in parts
        ]
        acc = norms[0]
        for norm, s in zip(norms[1:], scales[1:]):
            acc = acc + (norm - norms[0]) * spread_rows((s * inv)[h * n : (h + 1) * n, :])
        outs.append(acc)
    return outs, lse


def shard_kernel(first, n, q, keys, values, *refs):
    o = refs[-1]
    attend([q], keys, values, first, n, o)
    if len(refs) > 1:
        o[o.shape[0] - refs[0].shape[0] :] = refs[0][...]


def straight_kernel(owner, first, n, q, keys, values, fresh_k, fresh_v, o):
    place = lax.axis_index("ctx")
    sees = owner(place) > place

    @pl.when(sees)
    def _():
        attend([q], keys, values, first, n, o, (fresh_k, fresh_v))

    @pl.when(jnp.logical_not(sees))
    def _():
        attend([q], keys, values, first, n, o)


def sibling_kernel(tokens, qk, qv, keys, values, o):
    attend([qk, qv], keys, values, 0, tokens, o)


def own_kernel(tokens, qk, qv, keys, values, fresh_k, fresh_v, o):
    core = lax.axis_index("ctx") % CORES
    attend([qk, qv], keys, values, 0, tokens, o, (fresh_k, fresh_v), core * tokens)


def chip_sum_kernel(group, n, a, b, o):
    heads, hd = o.shape[1:]
    outs, lse = blend([(x[0:n], get_lse(x, n)) for x in (a, b)], group)
    for h, x in enumerate(outs):
        o[0:n, h * group : (h + 1) * group, :] = x.astype(BF16).reshape(n, group, hd)
    put_lse(o, n, lse)
    used = packed_shape(n, heads, hd).shape[0]
    if o.shape[0] > used:
        o[used:] = jnp.zeros((o.shape[0] - used, heads, hd), BF16)


def cut_lse(lse, kv, first, n, tokens):
    per = lse.shape[0] // kv
    a, b = first * per // tokens, (first + n) * per // tokens
    return jnp.concatenate([lse[h * per + a : h * per + b] for h in range(kv)], axis=0)


def near_kernel(group, own, sib, o, l):
    tokens, heads, hd = o.shape
    sib = sib.at[pl.ds(sib.shape[0] - own.shape[0], own.shape[0])]
    outs, lse = blend([(x[0:tokens], get_lse(x, tokens)) for x in (own, sib)], group)
    for h, x in enumerate(outs):
        o[:, h * group : (h + 1) * group, :] = x.reshape(tokens, group, hd)
    l[...] = lse


def final_kernel(group, first, n, near, near_l, *refs):
    *far, o, rows, sem = refs
    far = far[: len(far) - (first > 0)]
    tokens, heads, hd = o.shape
    lse = cut_lse(near_l[...], heads // group, first, n, tokens)
    parts = [(near[first : first + n], lse)] + [(x[0:n], get_lse(x, n)) for x in far]
    outs, _ = blend(parts, group)
    for h, x in enumerate(outs):
        rows[:, h * group : (h + 1) * group, :] = x.astype(BF16).reshape(n, group, hd)
    copy = pltpu.make_async_copy(rows, o.at[first : first + n], sem)
    copy.start()
    copy.wait()


def per_device(queries, new_keys, new_values, cache_keys, cache_values, cache_len):
    tokens, heads, hd = queries.shape
    slots, kv, _ = cache_keys.shape
    group = heads // kv
    n = lax.axis_size("ctx")
    chips = n // CORES
    unit = max(1, 128 // group)
    late = max(unit, tokens // 2 // unit * unit)
    shares = [(0, tokens - late), (tokens - late, late)]

    def over_core(x):
        return lax.ppermute(x, "ctx", [(i, i ^ 1) for i in range(n)])

    def over_chip(x, step):
        return lax.ppermute(x, "ctx", [(i, (i // CORES + step) % chips * CORES + i % CORES) for i in range(n)])

    def packed(m):
        return packed_shape(m, heads, hd)

    def cost(m):
        return pl.CostEstimate(
            flops=8 * m * heads * slots * hd, bytes_accessed=4 * 2**20, transcendentals=m * heads * slots
        )

    def call(name, kernel, out, args, estimate):
        return pl.pallas_call(
            kernel,
            out_shape=out,
            in_specs=[VMEM] * len(args),
            out_specs=jax.tree.map(lambda _: VMEM, out),
            compiler_params=params(),
            cost_estimate=estimate,
            name=name,
        )(*args)

    tiny = pl.CostEstimate(flops=0, bytes_accessed=0, transcendentals=0)
    small = pl.CostEstimate(flops=2**20, bytes_accessed=2**20, transcendentals=2**14)
    q_chip = [over_chip(queries, step) for step in range(1, chips)]
    fresh_rows = (tokens * kv // heads, heads, hd)
    moved = (cache_keys, cache_values, queries, new_keys.reshape(fresh_rows), new_values.reshape(fresh_rows))
    m = tokens // 2
    piece = jax.ShapeDtypeStruct((m + fresh_rows[0], heads, hd), BF16)
    k, v, qk, qv, filled = pl.pallas_call(
        load_kernel,
        out_shape=[
            jax.ShapeDtypeStruct(cache_keys.shape, BF16),
            jax.ShapeDtypeStruct(cache_values.shape, BF16),
            piece,
            piece,
            jax.ShapeDtypeStruct((8, hd), jnp.int32),
        ],
        in_specs=[pl.BlockSpec(memory_space=pl.ANY)] + [HBM] * len(moved),
        out_specs=[VMEM] * 5,
        scratch_shapes=[pltpu.SMEM((1,), jnp.int32), pltpu.SemaphoreType.DMA((7,))],
        compiler_params=params(),
        cost_estimate=tiny,
        name="load",
    )(cache_len, *[pltpu.with_memory_space_constraint(x, pltpu.HBM) for x in moved])
    qk_core, qv_core = over_core(qk), over_core(qv)
    keys, values = call(
        "prepare",
        functools.partial(prepare_kernel, m),
        [jax.ShapeDtypeStruct((kv, slots, hd), BF16), jax.ShapeDtypeStruct((kv, slots, 2 * hd), BF16)],
        (filled, k, v, qk),
        tiny,
    )
    shard = (keys, values)
    fresh = pl.pallas_call(
        functools.partial(fresh_kernel, m),
        out_shape=[
            jax.ShapeDtypeStruct((kv, CORES * tokens, hd), BF16),
            jax.ShapeDtypeStruct((kv, CORES * tokens, 2 * hd), BF16),
        ],
        in_specs=[VMEM] * 4,
        out_specs=[VMEM] * 2,
        scratch_shapes=[pltpu.VMEM((tokens * kv, hd), F32)],
        compiler_params=params(),
        cost_estimate=tiny,
        name="fresh",
    )(qk, qv, qk_core, qv_core)
    qk_core, *fresh = lax.optimization_barrier((qk_core, *fresh))

    def attend_part(name, kernel, m, *args):
        return call(name, kernel, packed(m), args, cost(m))

    kernel = functools.partial(sibling_kernel, tokens)
    sib = call("sibling", kernel, packed(tokens), (qk_core, qv_core, *shard), tiny)
    *q_chip, sib = lax.optimization_barrier((*q_chip, sib))
    q_diag = [over_core(q) for q in q_chip]
    far = []
    for step in range(1, chips):
        def owner(i, step=step):
            return (i // CORES - step + chips) % chips * CORES + i % CORES

        def straight_part(q, first, m):
            kernel = functools.partial(straight_kernel, owner, first, m)
            return call("straight", kernel, packed(m), (q, *shard, *fresh), tiny if first else cost(m))

        q_s, q_d = q_chip[step - 1], q_diag[step - 1]
        early = straight_part(q_s, *shares[0])
        q_d, early = lax.optimization_barrier((q_d, early))
        diag = []
        for first, m in shares:
            more = [sib] if first == 0 and step == 1 else []
            kernel = functools.partial(shard_kernel, first, m)
            shape = extended(packed(m), sum(x.shape[0] for x in more))
            diag.append(call("diagonal", kernel, shape, (q_d, *shard, *more), cost(m)))
            q_d, diag[-1] = lax.optimization_barrier((q_d, diag[-1]))
        q_s, diag[-1] = lax.optimization_barrier((q_s, diag[-1]))
        diag = [over_core(x) for x in diag]
        if step == 1:
            from_sib = diag[0]
        for i, (first, m) in enumerate(shares):
            straight = straight_part(q_s, first, m) if i else early
            shape = extended(packed(m), len(shares) - 1 - i)
            both = call("chip_sum", functools.partial(chip_sum_kernel, group, m), shape, (diag[i], straight), tiny)
            q_s, both, qk = lax.optimization_barrier((q_s, both, qk))
            far.append(over_chip(both, chips - step))
    own = call("own", functools.partial(own_kernel, tokens), packed(tokens), (qk, qv, *shard, *fresh), tiny)
    near = call(
        "near",
        functools.partial(near_kernel, group),
        [jax.ShapeDtypeStruct(queries.shape, F32), jax.ShapeDtypeStruct((tokens * heads // 128, 128), F32)],
        (own, from_sib),
        tiny,
    )
    out = []
    for i, (first, n_tokens) in enumerate(shares):
        args = (*near, *far[i :: len(shares)], *out)
        out = [
            pl.pallas_call(
                functools.partial(final_kernel, group, first, n_tokens),
                out_shape=jax.ShapeDtypeStruct(queries.shape, BF16),
                in_specs=[VMEM] * (len(args) - len(out)) + [HBM] * len(out),
                out_specs=HBM,
                scratch_shapes=[pltpu.VMEM((n_tokens, heads, hd), BF16), pltpu.SemaphoreType.DMA],
                input_output_aliases={len(args) - 1: 0} if out else {},
                compiler_params=params(),
                cost_estimate=tiny,
                name="final",
            )(*args)
        ]
    return out[0]


def solution(mesh):
    spec = P(("conv", "ctx"), "head", None)
    return jax.shard_map(
        per_device,
        mesh=mesh,
        in_specs=(spec,) * 5 + (P("conv"),),
        out_specs=spec,
        check_vma=False,
    )
```

```python
import functools
import math

import jax
import jax.numpy as jnp
from jax import lax
from jax.experimental import pallas as pl
from jax.experimental.pallas import tpu as pltpu
from jax.sharding import PartitionSpec as P

NEG_FILL = -1e30
LOG2E = 1.4426950408889634
VMEM = pl.BlockSpec(memory_space=pltpu.VMEM)
SMEM = pl.BlockSpec(memory_space=pltpu.SMEM)
HBM = pl.BlockSpec(memory_space=pltpu.HBM)
F32 = jnp.float32
BF16 = jnp.bfloat16
NT = (((1,), (1,)), ((), ()))
CORES = 2


def params():
    return pltpu.CompilerParams(vmem_limit_bytes=36 * 2**20)


def pack_rows(wide):
    eye = lax.broadcasted_iota(jnp.int32, (128, 128), 0) == lax.broadcasted_iota(jnp.int32, (128, 128), 1)
    return jnp.concatenate(
        [
            jnp.sum(jnp.where(eye, wide[i * 128 : (i + 1) * 128], 0.0), axis=0, keepdims=True)
            for i in range(wide.shape[0] // 128)
        ],
        axis=0,
    )


def spread_rows(packed):
    return jnp.concatenate(
        [jnp.transpose(jnp.broadcast_to(packed[i : i + 1, :], (128, 128))) for i in range(packed.shape[0])], axis=0
    )


def load_kernel(k, v, q, nk, nv, k_out, v_out, q_out, new, sems):
    m = nk.shape[0]
    moves = [(k, k_out), (v, v_out), (q, q_out), (nk, new.at[0:m]), (nv, new.at[m:])]
    copies = [pltpu.make_async_copy(a, b, sems.at[i]) for i, (a, b) in enumerate(moves)]
    for c in copies[::-1]:
        c.start()
    for c in copies:
        c.wait()


def prepare_kernel(k, v, keys, values, at=0):
    slots, kv, hd = k.shape
    keys[:, at : at + slots] = jnp.swapaxes(k[...], 0, 1)
    values[:, at : at + slots, 0:hd] = jnp.swapaxes(v[...], 0, 1)
    values[:, at : at + slots, hd:] = jnp.ones((kv, slots, hd), BF16)


def exclude(count, at, slots, fill, keys, values):
    kv, _, hd = keys.shape
    cut = slice(at, at + slots)

    @pl.when(count < slots)
    def _():
        included = lax.broadcasted_iota(jnp.int32, (slots, hd), 0) < count
        for h in range(kv):
            keys[h, cut] = jnp.where(included, keys[h, cut].astype(F32), fill(h)).astype(BF16)
            values[h, cut, 0:hd] = jnp.where(included, values[h, cut, 0:hd].astype(F32), 0.0).astype(BF16)
            values[h, cut, hd:] = jnp.where(included, 1.0, 0.0).astype(BF16)


def own_shard_kernel(slots, length, new, _k, _v, keys, values):
    count = jnp.clip(length[0] - lax.axis_index("ctx") * slots, 0, slots)
    first_new = new[0].astype(F32)

    def fill(h):
        return jnp.where(count > 0, keys[h, 0:1, :].astype(F32), first_new[h : h + 1])

    exclude(count, 0, slots, fill, keys, values)


def other_shard_kernel(length, k, v, new, new_core, _k, _v, keys, values, rows):
    slots, kv, hd = k.shape
    prepare_kernel(k, v, keys, values, slots)
    place = lax.axis_index("ctx")
    low = place % CORES == 0
    m = new.shape[0] // 2
    tokens = rows.shape[0] // kv
    end = 2 * slots
    for j, out in enumerate((keys, values)):
        mine, other = [x[j * m : (j + 1) * m].astype(F32) for x in (new, new_core)]
        for i, x in enumerate((jnp.where(low, mine, other), jnp.where(low, other, mine))):
            rows[...] = x.reshape(tokens * kv, hd)
            first = end + i * tokens
            for h in range(kv):
                out[h, first : first + tokens, 0:hd] = rows[pl.ds(h, tokens, stride=kv), :].astype(BF16)
    values[:, end:, hd:] = jnp.ones((kv, CORES * tokens, hd), BF16)
    count = jnp.clip(length[0] - place * slots, 0, slots)
    other_count = jnp.clip(length[0] - (place ^ 1) * slots, 0, slots)

    def fill(h):
        own, other, new_key = [keys[h, i : i + 1, :].astype(F32) for i in (0, slots, end)]
        return jnp.where(other_count > 0, other, jnp.where(count > 0, own, new_key))

    exclude(other_count, slots, slots, fill, keys, values)

    @pl.when(count == 0)
    def _():
        for h in range(kv):
            keys[h, 0:slots] = jnp.broadcast_to(fill(h), (slots, hd)).astype(BF16)


def put_lse(ref, first, lse):
    heads = ref.shape[1]
    high = lse.astype(BF16).astype(F32)
    middle = (lse - high).astype(BF16).astype(F32)
    low = lse - high - middle
    extra = lse_rows(lse.shape[0], heads)
    rest = jnp.zeros((extra * heads - 3 * lse.shape[0], 128), F32)
    rows = jnp.concatenate([high, middle, low, rest], axis=0)
    ref[first : first + extra] = rows.astype(BF16).reshape(extra, heads, 128)


def lse_rows(n, heads):
    return -(-3 * n // heads)


def get_lse(ref, first):
    heads = ref.shape[1]
    n = first * heads // 128
    extra = lse_rows(n, heads)
    rows = ref[first : first + extra].astype(F32).reshape(extra * heads, 128)
    return rows[0:n] + rows[n : 2 * n] + rows[2 * n : 3 * n]


def packed_shape(tokens, heads, hd):
    return jax.ShapeDtypeStruct((tokens + lse_rows(tokens * heads // 128, heads), heads, hd), BF16)


def extended(shape, rows):
    return jax.ShapeDtypeStruct((shape.shape[0] + rows,) + shape.shape[1:], shape.dtype)


def attend(q_ref, keys, values, cuts, first, n, o_ref, causal=None):
    heads, hd = q_ref.shape[1:]
    kv = keys.shape[0]
    group = heads // kv
    rows = n * group
    scale = LOG2E / math.sqrt(hd)
    if causal is not None:
        count = cuts[-1].stop - cuts[-1].start
        token = causal + lax.broadcasted_iota(jnp.int32, (rows, count), 0) // group
        seen = token >= lax.broadcasted_iota(jnp.int32, (rows, count), 1)

    def scores(h):
        q = q_ref[first : first + n, h * group : (h + 1) * group, :].reshape(rows, hd)
        found = [lax.dot_general(q, keys[h, cut], NT, preferred_element_type=F32) for cut in cuts]
        if causal is not None:
            found[-1] = jnp.where(seen, found[-1], NEG_FILL)
        return found

    now = scores(0)
    lses = []
    for h in range(kv):
        later = scores(h + 1) if h + 1 < kv else None
        peak = functools.reduce(jnp.maximum, [jnp.max(s, axis=-1, keepdims=True) for s in now])
        weights = [jnp.exp2((s - peak) * scale) for s in now]
        if causal is not None:
            weights[-1] = jnp.where(seen, weights[-1], 0.0)
        out = None
        for w, cut in zip(weights, cuts):
            term = jnp.dot(w.astype(BF16), values[h, cut], preferred_element_type=F32)
            out = term if out is None else out + term
        total = out[:, hd:]
        floored = jnp.maximum(total, 1.0)
        o_ref[0:n, h * group : (h + 1) * group, :] = (out[:, 0:hd] / floored).astype(BF16).reshape(n, group, hd)
        lses.append(pack_rows(jnp.where(total > 0.0, peak * (1.0 / math.sqrt(hd)) + jnp.log(floored), NEG_FILL)))
        now = later
    put_lse(o_ref, n, jnp.concatenate(lses, axis=0))
    used = packed_shape(n, heads, hd).shape[0]
    if o_ref.shape[0] > used:
        o_ref[used:] = jnp.zeros((o_ref.shape[0] - used, heads, hd), BF16)


def blend(parts, group):
    tokens, heads, hd = parts[0][0].shape
    top = functools.reduce(jnp.maximum, [lse for _, lse in parts])
    scales = [jnp.exp(lse - top) for _, lse in parts]
    total = functools.reduce(jnp.add, scales)
    lse = jnp.where(top > 0.5 * NEG_FILL, top + jnp.log(total), NEG_FILL)
    inv = 1.0 / total
    n = tokens * group // 128
    outs = []
    for h in range(heads // group):
        norms = [
            norm[:, h * group : (h + 1) * group, :].reshape(tokens * group, hd).astype(F32) for norm, _ in parts
        ]
        acc = norms[0]
        for norm, s in zip(norms[1:], scales[1:]):
            acc = acc + (norm - norms[0]) * spread_rows((s * inv)[h * n : (h + 1) * n, :])
        outs.append(acc)
    return outs, lse


def own_near_kernel(slots, q, keys, values, o):
    attend(q, keys, values, [slice(0, slots)], 0, q.shape[0], o)


def own_rest_kernel(slots, length, q, keys, values, o):
    tokens = q.shape[0]
    place = lax.axis_index("ctx")
    other, fresh = slice(slots, 2 * slots), slice(2 * slots, keys.shape[1])
    filled = length[0] > (place ^ 1) * slots

    @pl.when(filled)
    def _():
        attend(q, keys, values, [other, fresh], 0, tokens, o, place % CORES * tokens)

    @pl.when(jnp.logical_not(filled))
    def _():
        attend(q, keys, values, [fresh], 0, tokens, o, place % CORES * tokens)


def visitor_kernel(owner, slots, first, n, q, keys, values, o):
    place = lax.axis_index("ctx")
    sees = owner(place) > place

    @pl.when(sees)
    def _():
        attend(q, keys, values, [slice(0, keys.shape[1])], first, n, o)

    @pl.when(jnp.logical_not(sees))
    def _():
        attend(q, keys, values, [slice(0, 2 * slots)], first, n, o)


def cut_lse(lse, kv, first, n, tokens):
    per = lse.shape[0] // kv
    a, b = first * per // tokens, (first + n) * per // tokens
    return jnp.concatenate([lse[h * per + a : h * per + b] for h in range(kv)], axis=0)


def near_kernel(group, near, rest, o, l):
    tokens, heads, hd = o.shape
    outs, lse = blend([(x[0:tokens], get_lse(x, tokens)) for x in (near, rest)], group)
    for h, x in enumerate(outs):
        o[:, h * group : (h + 1) * group, :] = x.reshape(tokens, group, hd)
    l[...] = lse


def final_kernel(group, first, n, near, near_l, *refs):
    *far, o, rows, sem = refs
    far = far[: len(far) - (first > 0)]
    tokens, heads, hd = o.shape
    lse = cut_lse(near_l[...], heads // group, first, n, tokens)
    parts = [(near[first : first + n], lse)] + [(x[0:n], get_lse(x, n)) for x in far]
    outs, _ = blend(parts, group)
    for h, x in enumerate(outs):
        rows[:, h * group : (h + 1) * group, :] = x.astype(BF16).reshape(n, group, hd)
    copy = pltpu.make_async_copy(rows, o.at[first : first + n], sem)
    copy.start()
    copy.wait()


def per_device(queries, new_keys, new_values, cache_keys, cache_values, cache_len):
    tokens, heads, hd = queries.shape
    slots, kv, _ = cache_keys.shape
    group = heads // kv
    n = lax.axis_size("ctx")
    chips = n // CORES
    unit = max(1, 128 // group)
    late = max(unit, tokens // 2 // unit * unit)
    shares = [(0, tokens - late), (tokens - late, late)]

    def over_core(x):
        return lax.ppermute(x, "ctx", [(i, i ^ 1) for i in range(n)])

    def over_chip(x, step):
        return lax.ppermute(x, "ctx", [(i, (i // CORES + step) % chips * CORES + i % CORES) for i in range(n)])

    def packed(m):
        return packed_shape(m, heads, hd)

    def cost(m):
        return pl.CostEstimate(
            flops=8 * m * heads * slots * hd, bytes_accessed=4 * 2**20, transcendentals=m * heads * slots
        )

    def call(name, kernel, out, args, estimate):
        return pl.pallas_call(
            kernel,
            out_shape=out,
            in_specs=[VMEM] * len(args),
            out_specs=jax.tree.map(lambda _: VMEM, out),
            compiler_params=params(),
            cost_estimate=estimate,
            name=name,
        )(*args)

    tiny = pl.CostEstimate(flops=0, bytes_accessed=0, transcendentals=0)
    small = pl.CostEstimate(flops=2**20, bytes_accessed=2**20, transcendentals=2**14)
    q_chip = [over_chip(queries, step) for step in range(1, chips)]
    k_core, v_core = over_core(cache_keys), over_core(cache_values)
    new_rows = (tokens * kv // heads, heads, hd)
    moved = (cache_keys, cache_values, queries, new_keys.reshape(new_rows), new_values.reshape(new_rows))
    out = [jax.ShapeDtypeStruct(x.shape, BF16) for x in moved[:3]]
    out.append(jax.ShapeDtypeStruct((2 * new_rows[0], heads, hd), BF16))
    k, v, q_own, new = pl.pallas_call(
        load_kernel,
        out_shape=out,
        in_specs=[HBM] * len(moved),
        out_specs=[VMEM] * len(out),
        scratch_shapes=[pltpu.SemaphoreType.DMA((len(moved),))],
        compiler_params=params(),
        cost_estimate=tiny,
        name="load",
    )(*[pltpu.with_memory_space_constraint(x, pltpu.HBM) for x in moved])
    new_core = over_core(new)
    places = 2 * slots + CORES * tokens
    both = [jax.ShapeDtypeStruct((kv, places, hd), BF16), jax.ShapeDtypeStruct((kv, places, 2 * hd), BF16)]
    keys, values = call("prepare", prepare_kernel, both, (k, v), tiny)
    keys, values = pl.pallas_call(
        functools.partial(own_shard_kernel, slots),
        out_shape=both,
        in_specs=[SMEM] + [VMEM] * 3,
        out_specs=[VMEM] * 2,
        input_output_aliases={2: 0, 3: 1},
        compiler_params=params(),
        cost_estimate=tiny,
        name="own_shard",
    )(cache_len, new, keys, values)
    kernel = functools.partial(own_near_kernel, slots)
    own_near = call("own_near", kernel, packed(tokens), (q_own, keys, values), tiny)
    k_core, v_core, own_near = lax.optimization_barrier((k_core, v_core, own_near))
    keys, values = pl.pallas_call(
        other_shard_kernel,
        out_shape=both,
        in_specs=[SMEM] + [VMEM] * 6,
        out_specs=[VMEM] * 2,
        scratch_shapes=[pltpu.VMEM((tokens * kv, hd), F32)],
        input_output_aliases={5: 0, 6: 1},
        compiler_params=params(),
        cost_estimate=tiny,
        name="other_shard",
    )(cache_len, k_core, v_core, new, new_core, keys, values)
    far = []
    for step in range(1, chips):
        def owner(i, step=step):
            return (i // CORES - step + chips) % chips * CORES + i % CORES

        q = q_chip[step - 1]
        for i, (first, m) in enumerate(shares):
            kernel = functools.partial(visitor_kernel, owner, slots, first, m)
            shape = extended(packed(m), len(shares) - 1 - i)
            part = call("visitor", kernel, shape, (q, keys, values), tiny if i else cost(m))
            q, q_own, part = lax.optimization_barrier((q, q_own, part))
            far.append(over_chip(part, chips - step))
    own_rest = pl.pallas_call(
        functools.partial(own_rest_kernel, slots),
        out_shape=packed(tokens),
        in_specs=[SMEM] + [VMEM] * 3,
        out_specs=VMEM,
        compiler_params=params(),
        cost_estimate=tiny,
        name="own_rest",
    )(cache_len, q_own, keys, values)
    near = call(
        "near",
        functools.partial(near_kernel, group),
        [jax.ShapeDtypeStruct(queries.shape, F32), jax.ShapeDtypeStruct((tokens * heads // 128, 128), F32)],
        (own_near, own_rest),
        tiny,
    )
    out = []
    for i, (first, n_tokens) in enumerate(shares):
        args = (*near, *far[i :: len(shares)], *out)
        out = [
            pl.pallas_call(
                functools.partial(final_kernel, group, first, n_tokens),
                out_shape=jax.ShapeDtypeStruct(queries.shape, BF16),
                in_specs=[VMEM] * (len(args) - len(out)) + [HBM] * len(out),
                out_specs=HBM,
                scratch_shapes=[pltpu.VMEM((n_tokens, heads, hd), BF16), pltpu.SemaphoreType.DMA],
                input_output_aliases={len(args) - 1: 0} if out else {},
                compiler_params=params(),
                cost_estimate=tiny,
                name="final",
            )(*args)
        ]
    return out[0]


def solution(mesh):
    spec = P(("conv", "ctx"), "head", None)
    return jax.shard_map(
        per_device,
        mesh=mesh,
        in_specs=(spec,) * 5 + (P("conv"),),
        out_specs=spec,
        check_vma=False,
    )
```

```python
import functools
import math

import jax
import jax.numpy as jnp
from jax import lax
from jax.experimental import pallas as pl
from jax.experimental.pallas import tpu as pltpu
from jax.sharding import PartitionSpec as P

NEG_FILL = -1e30
LOG2E = 1.4426950408889634
VMEM = pl.BlockSpec(memory_space=pltpu.VMEM)
SMEM = pl.BlockSpec(memory_space=pltpu.SMEM)
HBM = pl.BlockSpec(memory_space=pltpu.HBM)
F32 = jnp.float32
BF16 = jnp.bfloat16
NT = (((1,), (1,)), ((), ()))
CORES = 2


def params():
    return pltpu.CompilerParams(vmem_limit_bytes=36 * 2**20)


def pack_rows(wide):
    eye = lax.broadcasted_iota(jnp.int32, (128, 128), 0) == lax.broadcasted_iota(jnp.int32, (128, 128), 1)
    return jnp.concatenate(
        [
            jnp.sum(jnp.where(eye, wide[i * 128 : (i + 1) * 128], 0.0), axis=0, keepdims=True)
            for i in range(wide.shape[0] // 128)
        ],
        axis=0,
    )


def spread_rows(packed):
    return jnp.concatenate(
        [jnp.transpose(jnp.broadcast_to(packed[i : i + 1, :], (128, 128))) for i in range(packed.shape[0])], axis=0
    )


def load_kernel(k, v, q, nk, nv, k_out, v_out, q_out, new, sems):
    m = nk.shape[0]
    moves = [(k, k_out), (v, v_out), (q, q_out), (nk, new.at[0:m]), (nv, new.at[m:])]
    copies = [pltpu.make_async_copy(a, b, sems.at[i]) for i, (a, b) in enumerate(moves)]
    for c in copies[::-1]:
        c.start()
    for c in copies:
        c.wait()


def prepare_kernel(k, v, keys, values, at=0):
    slots, kv, hd = k.shape
    keys[:, at : at + slots] = jnp.swapaxes(k[...], 0, 1)
    values[:, at : at + slots, 0:hd] = jnp.swapaxes(v[...], 0, 1)
    values[:, at : at + slots, hd:] = jnp.ones((kv, slots, hd), BF16)


def exclude(count, at, slots, fill, keys, values):
    kv, _, hd = keys.shape
    cut = slice(at, at + slots)

    @pl.when(count < slots)
    def _():
        included = lax.broadcasted_iota(jnp.int32, (slots, hd), 0) < count
        for h in range(kv):
            keys[h, cut] = jnp.where(included, keys[h, cut].astype(F32), fill(h)).astype(BF16)
            values[h, cut, 0:hd] = jnp.where(included, values[h, cut, 0:hd].astype(F32), 0.0).astype(BF16)
            values[h, cut, hd:] = jnp.where(included, 1.0, 0.0).astype(BF16)


def own_shard_kernel(slots, length, new, _k, _v, keys, values):
    count = jnp.clip(length[0] - lax.axis_index("ctx") * slots, 0, slots)
    first_new = new[0].astype(F32)

    def fill(h):
        return jnp.where(count > 0, keys[h, 0:1, :].astype(F32), first_new[h : h + 1])

    exclude(count, 0, slots, fill, keys, values)


def other_shard_kernel(length, k, v, new, new_core, _k, _v, keys, values, rows):
    slots, kv, hd = k.shape
    prepare_kernel(k, v, keys, values, slots)
    place = lax.axis_index("ctx")
    low = place % CORES == 0
    m = new.shape[0] // 2
    tokens = rows.shape[0] // kv
    end = 2 * slots
    for j, out in enumerate((keys, values)):
        mine, other = [x[j * m : (j + 1) * m].astype(F32) for x in (new, new_core)]
        for i, x in enumerate((jnp.where(low, mine, other), jnp.where(low, other, mine))):
            rows[...] = x.reshape(tokens * kv, hd)
            first = end + i * tokens
            for h in range(kv):
                out[h, first : first + tokens, 0:hd] = rows[pl.ds(h, tokens, stride=kv), :].astype(BF16)
    values[:, end:, hd:] = jnp.ones((kv, CORES * tokens, hd), BF16)
    count = jnp.clip(length[0] - place * slots, 0, slots)
    other_count = jnp.clip(length[0] - (place ^ 1) * slots, 0, slots)

    def fill(h):
        own, other, new_key = [keys[h, i : i + 1, :].astype(F32) for i in (0, slots, end)]
        return jnp.where(other_count > 0, other, jnp.where(count > 0, own, new_key))

    exclude(other_count, slots, slots, fill, keys, values)

    @pl.when(count == 0)
    def _():
        for h in range(kv):
            keys[h, 0:slots] = jnp.broadcast_to(fill(h), (slots, hd)).astype(BF16)


def put_lse(ref, first, lse):
    heads = ref.shape[1]
    high = lse.astype(BF16).astype(F32)
    middle = (lse - high).astype(BF16).astype(F32)
    low = lse - high - middle
    extra = lse_rows(lse.shape[0], heads)
    rest = jnp.zeros((extra * heads - 3 * lse.shape[0], 128), F32)
    rows = jnp.concatenate([high, middle, low, rest], axis=0)
    ref[first : first + extra] = rows.astype(BF16).reshape(extra, heads, 128)


def lse_rows(n, heads):
    return -(-3 * n // heads)


def get_lse(ref, first):
    heads = ref.shape[1]
    n = first * heads // 128
    extra = lse_rows(n, heads)
    rows = ref[first : first + extra].astype(F32).reshape(extra * heads, 128)
    return rows[0:n] + rows[n : 2 * n] + rows[2 * n : 3 * n]


def packed_shape(tokens, heads, hd):
    return jax.ShapeDtypeStruct((tokens + lse_rows(tokens * heads // 128, heads), heads, hd), BF16)


def extended(shape, rows):
    return jax.ShapeDtypeStruct((shape.shape[0] + rows,) + shape.shape[1:], shape.dtype)


def attend(q_ref, keys, values, cuts, first, n, o_ref, causal=None):
    heads, hd = q_ref.shape[1:]
    kv = keys.shape[0]
    group = heads // kv
    rows = n * group
    scale = LOG2E / math.sqrt(hd)
    if causal is not None:
        count = cuts[-1].stop - cuts[-1].start
        token = causal + lax.broadcasted_iota(jnp.int32, (rows, count), 0) // group
        seen = token >= lax.broadcasted_iota(jnp.int32, (rows, count), 1)

    def scores(h):
        q = q_ref[first : first + n, h * group : (h + 1) * group, :].reshape(rows, hd)
        found = [lax.dot_general(q, keys[h, cut], NT, preferred_element_type=F32) for cut in cuts]
        if causal is not None:
            found[-1] = jnp.where(seen, found[-1], NEG_FILL)
        return found

    now = scores(0)
    lses = []
    for h in range(kv):
        later = scores(h + 1) if h + 1 < kv else None
        peak = functools.reduce(jnp.maximum, [jnp.max(s, axis=-1, keepdims=True) for s in now])
        weights = [jnp.exp2((s - peak) * scale) for s in now]
        if causal is not None:
            weights[-1] = jnp.where(seen, weights[-1], 0.0)
        out = None
        for w, cut in zip(weights, cuts):
            term = jnp.dot(w.astype(BF16), values[h, cut], preferred_element_type=F32)
            out = term if out is None else out + term
        total = out[:, hd:]
        floored = jnp.maximum(total, 1.0)
        o_ref[0:n, h * group : (h + 1) * group, :] = (out[:, 0:hd] / floored).astype(BF16).reshape(n, group, hd)
        lses.append(pack_rows(jnp.where(total > 0.0, peak * (1.0 / math.sqrt(hd)) + jnp.log(floored), NEG_FILL)))
        now = later
    put_lse(o_ref, n, jnp.concatenate(lses, axis=0))
    used = packed_shape(n, heads, hd).shape[0]
    if o_ref.shape[0] > used:
        o_ref[used:] = jnp.zeros((o_ref.shape[0] - used, heads, hd), BF16)


def blend(parts, group):
    tokens, heads, hd = parts[0][0].shape
    top = functools.reduce(jnp.maximum, [lse for _, lse in parts])
    scales = [jnp.exp(lse - top) for _, lse in parts]
    total = functools.reduce(jnp.add, scales)
    lse = jnp.where(top > 0.5 * NEG_FILL, top + jnp.log(total), NEG_FILL)
    inv = 1.0 / total
    n = tokens * group // 128
    outs = []
    for h in range(heads // group):
        norms = [
            norm[:, h * group : (h + 1) * group, :].reshape(tokens * group, hd).astype(F32) for norm, _ in parts
        ]
        acc = norms[0]
        for norm, s in zip(norms[1:], scales[1:]):
            acc = acc + (norm - norms[0]) * spread_rows((s * inv)[h * n : (h + 1) * n, :])
        outs.append(acc)
    return outs, lse


def own_near_kernel(slots, q, keys, values, o):
    attend(q, keys, values, [slice(0, slots)], 0, q.shape[0], o)


def own_rest_kernel(slots, length, q, keys, values, o):
    tokens = q.shape[0]
    place = lax.axis_index("ctx")
    other, fresh = slice(slots, 2 * slots), slice(2 * slots, keys.shape[1])
    filled = length[0] > (place ^ 1) * slots

    @pl.when(filled)
    def _():
        attend(q, keys, values, [other, fresh], 0, tokens, o, place % CORES * tokens)

    @pl.when(jnp.logical_not(filled))
    def _():
        attend(q, keys, values, [fresh], 0, tokens, o, place % CORES * tokens)


def visitor_kernel(owner, slots, first, n, q, keys, values, o):
    place = lax.axis_index("ctx")
    sees = owner(place) > place

    @pl.when(sees)
    def _():
        attend(q, keys, values, [slice(0, keys.shape[1])], first, n, o)

    @pl.when(jnp.logical_not(sees))
    def _():
        attend(q, keys, values, [slice(0, 2 * slots)], first, n, o)


def cut_lse(lse, kv, first, n, tokens):
    per = lse.shape[0] // kv
    a, b = first * per // tokens, (first + n) * per // tokens
    return jnp.concatenate([lse[h * per + a : h * per + b] for h in range(kv)], axis=0)


def near_kernel(group, near, rest, o, l):
    tokens, heads, hd = o.shape
    outs, lse = blend([(x[0:tokens], get_lse(x, tokens)) for x in (near, rest)], group)
    for h, x in enumerate(outs):
        o[:, h * group : (h + 1) * group, :] = x.reshape(tokens, group, hd)
    l[...] = lse


def final_kernel(group, first, n, near, near_l, *refs):
    *far, o, rows, sem = refs
    far = far[: len(far) - (first > 0)]
    tokens, heads, hd = o.shape
    lse = cut_lse(near_l[...], heads // group, first, n, tokens)
    parts = [(near[first : first + n], lse)] + [(x[0:n], get_lse(x, n)) for x in far]
    outs, _ = blend(parts, group)
    for h, x in enumerate(outs):
        rows[:, h * group : (h + 1) * group, :] = x.astype(BF16).reshape(n, group, hd)
    copy = pltpu.make_async_copy(rows, o.at[first : first + n], sem)
    copy.start()
    copy.wait()


def per_device(queries, new_keys, new_values, cache_keys, cache_values, cache_len):
    tokens, heads, hd = queries.shape
    slots, kv, _ = cache_keys.shape
    group = heads // kv
    n = lax.axis_size("ctx")
    chips = n // CORES
    unit = max(1, 128 // group)
    late = max(unit, tokens // 2 // unit * unit)
    shares = [(0, tokens - late), (tokens - late, late)]

    def over_core(x):
        return lax.ppermute(x, "ctx", [(i, i ^ 1) for i in range(n)])

    def over_chip(x, step):
        return lax.ppermute(x, "ctx", [(i, (i // CORES + step) % chips * CORES + i % CORES) for i in range(n)])

    def packed(m):
        return packed_shape(m, heads, hd)

    def cost(m):
        return pl.CostEstimate(
            flops=8 * m * heads * slots * hd, bytes_accessed=4 * 2**20, transcendentals=m * heads * slots
        )

    def call(name, kernel, out, args, estimate):
        return pl.pallas_call(
            kernel,
            out_shape=out,
            in_specs=[VMEM] * len(args),
            out_specs=jax.tree.map(lambda _: VMEM, out),
            compiler_params=params(),
            cost_estimate=estimate,
            name=name,
        )(*args)

    tiny = pl.CostEstimate(flops=0, bytes_accessed=0, transcendentals=0)
    small = pl.CostEstimate(flops=2**20, bytes_accessed=2**20, transcendentals=2**14)
    q_chip = [over_chip(queries, step) for step in range(1, chips)]
    new_rows = (tokens * kv // heads, heads, hd)
    moved = (cache_keys, cache_values, queries, new_keys.reshape(new_rows), new_values.reshape(new_rows))
    out = [jax.ShapeDtypeStruct(x.shape, BF16) for x in moved[:3]]
    out.append(jax.ShapeDtypeStruct((2 * new_rows[0], heads, hd), BF16))
    k, v, q_own, new = pl.pallas_call(
        load_kernel,
        out_shape=out,
        in_specs=[HBM] * len(moved),
        out_specs=[VMEM] * len(out),
        scratch_shapes=[pltpu.SemaphoreType.DMA((len(moved),))],
        compiler_params=params(),
        cost_estimate=tiny,
        name="load",
    )(*[pltpu.with_memory_space_constraint(x, pltpu.HBM) for x in moved])
    k_core, v_core = over_core(k), over_core(v)
    new_core = over_core(new)
    places = 2 * slots + CORES * tokens
    both = [jax.ShapeDtypeStruct((kv, places, hd), BF16), jax.ShapeDtypeStruct((kv, places, 2 * hd), BF16)]
    keys, values = call("prepare", prepare_kernel, both, (k, v), tiny)
    keys, values = pl.pallas_call(
        functools.partial(own_shard_kernel, slots),
        out_shape=both,
        in_specs=[SMEM] + [VMEM] * 3,
        out_specs=[VMEM] * 2,
        input_output_aliases={2: 0, 3: 1},
        compiler_params=params(),
        cost_estimate=tiny,
        name="own_shard",
    )(cache_len, new, keys, values)
    kernel = functools.partial(own_near_kernel, slots)
    own_near = call("own_near", kernel, packed(tokens), (q_own, keys, values), cost(tokens * 50))
    k_core, v_core, own_near = lax.optimization_barrier((k_core, v_core, own_near))
    keys, values = pl.pallas_call(
        other_shard_kernel,
        out_shape=both,
        in_specs=[SMEM] + [VMEM] * 6,
        out_specs=[VMEM] * 2,
        scratch_shapes=[pltpu.VMEM((tokens * kv, hd), F32)],
        input_output_aliases={5: 0, 6: 1},
        compiler_params=params(),
        cost_estimate=tiny,
        name="other_shard",
    )(cache_len, k_core, v_core, new, new_core, keys, values)
    far = []
    for step in range(1, chips):
        def owner(i, step=step):
            return (i // CORES - step + chips) % chips * CORES + i % CORES

        q = q_chip[step - 1]
        for i, (first, m) in enumerate(shares):
            kernel = functools.partial(visitor_kernel, owner, slots, first, m)
            shape = extended(packed(m), len(shares) - 1 - i)
            part = call("visitor", kernel, shape, (q, keys, values), tiny if i else cost(m))
            q, q_own, part = lax.optimization_barrier((q, q_own, part))
            far.append(over_chip(part, chips - step))
    own_rest = pl.pallas_call(
        functools.partial(own_rest_kernel, slots),
        out_shape=packed(tokens),
        in_specs=[SMEM] + [VMEM] * 3,
        out_specs=VMEM,
        compiler_params=params(),
        cost_estimate=tiny,
        name="own_rest",
    )(cache_len, q_own, keys, values)
    near = call(
        "near",
        functools.partial(near_kernel, group),
        [jax.ShapeDtypeStruct(queries.shape, F32), jax.ShapeDtypeStruct((tokens * heads // 128, 128), F32)],
        (own_near, own_rest),
        tiny,
    )
    out = []
    for i, (first, n_tokens) in enumerate(shares):
        args = (*near, *far[i :: len(shares)], *out)
        out = [
            pl.pallas_call(
                functools.partial(final_kernel, group, first, n_tokens),
                out_shape=jax.ShapeDtypeStruct(queries.shape, BF16),
                in_specs=[VMEM] * (len(args) - len(out)) + [HBM] * len(out),
                out_specs=HBM,
                scratch_shapes=[pltpu.VMEM((n_tokens, heads, hd), BF16), pltpu.SemaphoreType.DMA],
                input_output_aliases={len(args) - 1: 0} if out else {},
                compiler_params=params(),
                cost_estimate=tiny,
                name="final",
            )(*args)
        ]
    return out[0]


def solution(mesh):
    spec = P(("conv", "ctx"), "head", None)
    return jax.shard_map(
        per_device,
        mesh=mesh,
        in_specs=(spec,) * 5 + (P("conv"),),
        out_specs=spec,
        check_vma=False,
    )
```

```python
import functools
import math

import jax
import jax.numpy as jnp
from jax import lax
from jax.experimental import pallas as pl
from jax.experimental.pallas import tpu as pltpu
from jax.sharding import PartitionSpec as P

NEG_FILL = -1e30
LOG2E = 1.4426950408889634
VMEM = pl.BlockSpec(memory_space=pltpu.VMEM)
SMEM = pl.BlockSpec(memory_space=pltpu.SMEM)
HBM = pl.BlockSpec(memory_space=pltpu.HBM)
F32 = jnp.float32
BF16 = jnp.bfloat16
NT = (((1,), (1,)), ((), ()))
CORES = 2


def params():
    return pltpu.CompilerParams(vmem_limit_bytes=36 * 2**20)


def pack_rows(wide):
    eye = lax.broadcasted_iota(jnp.int32, (128, 128), 0) == lax.broadcasted_iota(jnp.int32, (128, 128), 1)
    return jnp.concatenate(
        [
            jnp.sum(jnp.where(eye, wide[i * 128 : (i + 1) * 128], 0.0), axis=0, keepdims=True)
            for i in range(wide.shape[0] // 128)
        ],
        axis=0,
    )


def spread_rows(packed):
    return jnp.concatenate(
        [jnp.transpose(jnp.broadcast_to(packed[i : i + 1, :], (128, 128))) for i in range(packed.shape[0])], axis=0
    )


def load_kernel(k, v, q, nk, nv, k_out, v_out, q_out, new, sems):
    m = nk.shape[0]
    moves = [(k, k_out), (v, v_out), (q, q_out), (nk, new.at[0:m]), (nv, new.at[m:])]
    copies = [pltpu.make_async_copy(a, b, sems.at[i]) for i, (a, b) in enumerate(moves)]
    for c in copies[::-1]:
        c.start()
    for c in copies:
        c.wait()


def prepare_kernel(k, v, keys, values, at=0):
    slots, kv, hd = k.shape
    keys[:, at : at + slots] = jnp.swapaxes(k[...], 0, 1)
    values[:, at : at + slots, 0:hd] = jnp.swapaxes(v[...], 0, 1)
    values[:, at : at + slots, hd:] = jnp.ones((kv, slots, hd), BF16)


def exclude(count, at, slots, fill, keys, values):
    kv, _, hd = keys.shape
    cut = slice(at, at + slots)

    @pl.when(count < slots)
    def _():
        included = lax.broadcasted_iota(jnp.int32, (slots, hd), 0) < count
        for h in range(kv):
            keys[h, cut] = jnp.where(included, keys[h, cut].astype(F32), fill(h)).astype(BF16)
            values[h, cut, 0:hd] = jnp.where(included, values[h, cut, 0:hd].astype(F32), 0.0).astype(BF16)
            values[h, cut, hd:] = jnp.where(included, 1.0, 0.0).astype(BF16)


def own_shard_kernel(length, k, v, new, keys, values):
    slots = k.shape[0]
    prepare_kernel(k, v, keys, values)
    count = jnp.clip(length[0] - lax.axis_index("ctx") * slots, 0, slots)
    first_new = new[0].astype(F32)

    def fill(h):
        return jnp.where(count > 0, keys[h, 0:1, :].astype(F32), first_new[h : h + 1])

    exclude(count, 0, slots, fill, keys, values)


def other_shard_kernel(length, k, v, new, new_core, _k, _v, keys, values, rows):
    slots, kv, hd = k.shape
    prepare_kernel(k, v, keys, values, slots)
    place = lax.axis_index("ctx")
    low = place % CORES == 0
    m = new.shape[0] // 2
    tokens = rows.shape[0] // kv
    end = 2 * slots
    for j, out in enumerate((keys, values)):
        mine, other = [x[j * m : (j + 1) * m].astype(F32) for x in (new, new_core)]
        for i, x in enumerate((jnp.where(low, mine, other), jnp.where(low, other, mine))):
            rows[...] = x.reshape(tokens * kv, hd)
            first = end + i * tokens
            for h in range(kv):
                out[h, first : first + tokens, 0:hd] = rows[pl.ds(h, tokens, stride=kv), :].astype(BF16)
    values[:, end:, hd:] = jnp.ones((kv, CORES * tokens, hd), BF16)
    count = jnp.clip(length[0] - place * slots, 0, slots)
    other_count = jnp.clip(length[0] - (place ^ 1) * slots, 0, slots)

    def fill(h):
        own, other, new_key = [keys[h, i : i + 1, :].astype(F32) for i in (0, slots, end)]
        return jnp.where(other_count > 0, other, jnp.where(count > 0, own, new_key))

    exclude(other_count, slots, slots, fill, keys, values)

    @pl.when(count == 0)
    def _():
        for h in range(kv):
            keys[h, 0:slots] = jnp.broadcast_to(fill(h), (slots, hd)).astype(BF16)


def put_lse(ref, first, lse):
    heads = ref.shape[1]
    high = lse.astype(BF16).astype(F32)
    middle = (lse - high).astype(BF16).astype(F32)
    low = lse - high - middle
    extra = lse_rows(lse.shape[0], heads)
    rest = jnp.zeros((extra * heads - 3 * lse.shape[0], 128), F32)
    rows = jnp.concatenate([high, middle, low, rest], axis=0)
    ref[first : first + extra] = rows.astype(BF16).reshape(extra, heads, 128)


def lse_rows(n, heads):
    return -(-3 * n // heads)


def get_lse(ref, first):
    heads = ref.shape[1]
    n = first * heads // 128
    extra = lse_rows(n, heads)
    rows = ref[first : first + extra].astype(F32).reshape(extra * heads, 128)
    return rows[0:n] + rows[n : 2 * n] + rows[2 * n : 3 * n]


def packed_shape(tokens, heads, hd):
    return jax.ShapeDtypeStruct((tokens + lse_rows(tokens * heads // 128, heads), heads, hd), BF16)


def extended(shape, rows):
    return jax.ShapeDtypeStruct((shape.shape[0] + rows,) + shape.shape[1:], shape.dtype)


def attend(q_ref, keys, values, cuts, first, n, o_ref, causal=None):
    heads, hd = q_ref.shape[1:]
    kv = keys.shape[0]
    group = heads // kv
    rows = n * group
    scale = LOG2E / math.sqrt(hd)
    if causal is not None:
        count = cuts[-1].stop - cuts[-1].start
        token = causal + lax.broadcasted_iota(jnp.int32, (rows, count), 0) // group
        seen = token >= lax.broadcasted_iota(jnp.int32, (rows, count), 1)

    def scores(h):
        q = q_ref[first : first + n, h * group : (h + 1) * group, :].reshape(rows, hd)
        found = [lax.dot_general(q, keys[h, cut], NT, preferred_element_type=F32) for cut in cuts]
        if causal is not None:
            found[-1] = jnp.where(seen, found[-1], NEG_FILL)
        return found

    now = scores(0)
    lses = []
    for h in range(kv):
        later = scores(h + 1) if h + 1 < kv else None
        peak = functools.reduce(jnp.maximum, [jnp.max(s, axis=-1, keepdims=True) for s in now])
        weights = [jnp.exp2((s - peak) * scale) for s in now]
        if causal is not None:
            weights[-1] = jnp.where(seen, weights[-1], 0.0)
        out = None
        for w, cut in zip(weights, cuts):
            term = jnp.dot(w.astype(BF16), values[h, cut], preferred_element_type=F32)
            out = term if out is None else out + term
        total = out[:, hd:]
        floored = jnp.maximum(total, 1.0)
        o_ref[0:n, h * group : (h + 1) * group, :] = (out[:, 0:hd] / floored).astype(BF16).reshape(n, group, hd)
        lses.append(pack_rows(jnp.where(total > 0.0, peak * (1.0 / math.sqrt(hd)) + jnp.log(floored), NEG_FILL)))
        now = later
    put_lse(o_ref, n, jnp.concatenate(lses, axis=0))
    used = packed_shape(n, heads, hd).shape[0]
    if o_ref.shape[0] > used:
        o_ref[used:] = jnp.zeros((o_ref.shape[0] - used, heads, hd), BF16)


def blend(parts, group):
    tokens, heads, hd = parts[0][0].shape
    top = functools.reduce(jnp.maximum, [lse for _, lse in parts])
    scales = [jnp.exp(lse - top) for _, lse in parts]
    total = functools.reduce(jnp.add, scales)
    lse = jnp.where(top > 0.5 * NEG_FILL, top + jnp.log(total), NEG_FILL)
    inv = 1.0 / total
    n = tokens * group // 128
    outs = []
    for h in range(heads // group):
        norms = [
            norm[:, h * group : (h + 1) * group, :].reshape(tokens * group, hd).astype(F32) for norm, _ in parts
        ]
        acc = norms[0]
        for norm, s in zip(norms[1:], scales[1:]):
            acc = acc + (norm - norms[0]) * spread_rows((s * inv)[h * n : (h + 1) * n, :])
        outs.append(acc)
    return outs, lse


def own_near_kernel(slots, q, keys, values, o):
    attend(q, keys, values, [slice(0, slots)], 0, q.shape[0], o)


def own_rest_kernel(slots, length, q, keys, values, o):
    tokens = q.shape[0]
    place = lax.axis_index("ctx")
    other, fresh = slice(slots, 2 * slots), slice(2 * slots, keys.shape[1])
    filled = length[0] > (place ^ 1) * slots

    @pl.when(filled)
    def _():
        attend(q, keys, values, [other, fresh], 0, tokens, o, place % CORES * tokens)

    @pl.when(jnp.logical_not(filled))
    def _():
        attend(q, keys, values, [fresh], 0, tokens, o, place % CORES * tokens)


def visitor_kernel(owner, slots, first, n, q, keys, values, o):
    place = lax.axis_index("ctx")
    sees = owner(place) > place

    @pl.when(sees)
    def _():
        attend(q, keys, values, [slice(0, keys.shape[1])], first, n, o)

    @pl.when(jnp.logical_not(sees))
    def _():
        attend(q, keys, values, [slice(0, 2 * slots)], first, n, o)


def cut_lse(lse, kv, first, n, tokens):
    per = lse.shape[0] // kv
    a, b = first * per // tokens, (first + n) * per // tokens
    return jnp.concatenate([lse[h * per + a : h * per + b] for h in range(kv)], axis=0)


def near_kernel(group, near, rest, o, l):
    tokens, heads, hd = o.shape
    outs, lse = blend([(x[0:tokens], get_lse(x, tokens)) for x in (near, rest)], group)
    for h, x in enumerate(outs):
        o[:, h * group : (h + 1) * group, :] = x.reshape(tokens, group, hd)
    l[...] = lse


def final_kernel(group, first, n, near, near_l, *refs):
    *far, o, rows, sem = refs
    far = far[: len(far) - (first > 0)]
    tokens, heads, hd = o.shape
    lse = cut_lse(near_l[...], heads // group, first, n, tokens)
    parts = [(near[first : first + n], lse)] + [(x[0:n], get_lse(x, n)) for x in far]
    outs, _ = blend(parts, group)
    for h, x in enumerate(outs):
        rows[:, h * group : (h + 1) * group, :] = x.astype(BF16).reshape(n, group, hd)
    copy = pltpu.make_async_copy(rows, o.at[first : first + n], sem)
    copy.start()
    copy.wait()


def per_device(queries, new_keys, new_values, cache_keys, cache_values, cache_len):
    tokens, heads, hd = queries.shape
    slots, kv, _ = cache_keys.shape
    group = heads // kv
    n = lax.axis_size("ctx")
    chips = n // CORES
    unit = max(1, 128 // group)
    late = max(unit, tokens // 2 // unit * unit)
    shares = [(0, tokens - late), (tokens - late, late)]

    def over_core(x):
        return lax.ppermute(x, "ctx", [(i, i ^ 1) for i in range(n)])

    def over_chip(x, step):
        return lax.ppermute(x, "ctx", [(i, (i // CORES + step) % chips * CORES + i % CORES) for i in range(n)])

    def packed(m):
        return packed_shape(m, heads, hd)

    def cost(m):
        return pl.CostEstimate(
            flops=8 * m * heads * slots * hd, bytes_accessed=4 * 2**20, transcendentals=m * heads * slots
        )

    def call(name, kernel, out, args, estimate):
        return pl.pallas_call(
            kernel,
            out_shape=out,
            in_specs=[VMEM] * len(args),
            out_specs=jax.tree.map(lambda _: VMEM, out),
            compiler_params=params(),
            cost_estimate=estimate,
            name=name,
        )(*args)

    tiny = pl.CostEstimate(flops=0, bytes_accessed=0, transcendentals=0)
    small = pl.CostEstimate(flops=2**20, bytes_accessed=2**20, transcendentals=2**14)
    q_chip = [over_chip(queries, step) for step in range(1, chips)]
    new_rows = (tokens * kv // heads, heads, hd)
    moved = (cache_keys, cache_values, queries, new_keys.reshape(new_rows), new_values.reshape(new_rows))
    out = [jax.ShapeDtypeStruct(x.shape, BF16) for x in moved[:3]]
    out.append(jax.ShapeDtypeStruct((2 * new_rows[0], heads, hd), BF16))
    k, v, q_own, new = pl.pallas_call(
        load_kernel,
        out_shape=out,
        in_specs=[HBM] * len(moved),
        out_specs=[VMEM] * len(out),
        scratch_shapes=[pltpu.SemaphoreType.DMA((len(moved),))],
        compiler_params=params(),
        cost_estimate=tiny,
        name="load",
    )(*[pltpu.with_memory_space_constraint(x, pltpu.HBM) for x in moved])
    k_core, v_core = over_core(k), over_core(v)
    new_core = over_core(new)
    places = 2 * slots + CORES * tokens
    both = [jax.ShapeDtypeStruct((kv, places, hd), BF16), jax.ShapeDtypeStruct((kv, places, 2 * hd), BF16)]
    keys, values = pl.pallas_call(
        own_shard_kernel,
        out_shape=both,
        in_specs=[SMEM] + [VMEM] * 3,
        out_specs=[VMEM] * 2,
        compiler_params=params(),
        cost_estimate=tiny,
        name="own_shard",
    )(cache_len, k, v, new)
    kernel = functools.partial(own_near_kernel, slots)
    own_near = call("own_near", kernel, packed(tokens), (q_own, keys, values), cost(tokens * 50))
    k_core, v_core, own_near = lax.optimization_barrier((k_core, v_core, own_near))
    keys, values = pl.pallas_call(
        other_shard_kernel,
        out_shape=both,
        in_specs=[SMEM] + [VMEM] * 6,
        out_specs=[VMEM] * 2,
        scratch_shapes=[pltpu.VMEM((tokens * kv, hd), F32)],
        input_output_aliases={5: 0, 6: 1},
        compiler_params=params(),
        cost_estimate=tiny,
        name="other_shard",
    )(cache_len, k_core, v_core, new, new_core, keys, values)
    far = []
    for step in range(1, chips):
        def owner(i, step=step):
            return (i // CORES - step + chips) % chips * CORES + i % CORES

        q = q_chip[step - 1]
        for i, (first, m) in enumerate(shares):
            kernel = functools.partial(visitor_kernel, owner, slots, first, m)
            shape = extended(packed(m), len(shares) - 1 - i)
            part = call("visitor", kernel, shape, (q, keys, values), tiny if i else cost(m))
            q, q_own, part = lax.optimization_barrier((q, q_own, part))
            far.append(over_chip(part, chips - step))
    own_rest = pl.pallas_call(
        functools.partial(own_rest_kernel, slots),
        out_shape=packed(tokens),
        in_specs=[SMEM] + [VMEM] * 3,
        out_specs=VMEM,
        compiler_params=params(),
        cost_estimate=tiny,
        name="own_rest",
    )(cache_len, q_own, keys, values)
    near = call(
        "near",
        functools.partial(near_kernel, group),
        [jax.ShapeDtypeStruct(queries.shape, F32), jax.ShapeDtypeStruct((tokens * heads // 128, 128), F32)],
        (own_near, own_rest),
        tiny,
    )
    out = []
    for i, (first, n_tokens) in enumerate(shares):
        args = (*near, *far[i :: len(shares)], *out)
        out = [
            pl.pallas_call(
                functools.partial(final_kernel, group, first, n_tokens),
                out_shape=jax.ShapeDtypeStruct(queries.shape, BF16),
                in_specs=[VMEM] * (len(args) - len(out)) + [HBM] * len(out),
                out_specs=HBM,
                scratch_shapes=[pltpu.VMEM((n_tokens, heads, hd), BF16), pltpu.SemaphoreType.DMA],
                input_output_aliases={len(args) - 1: 0} if out else {},
                compiler_params=params(),
                cost_estimate=tiny,
                name="final",
            )(*args)
        ]
    return out[0]


def solution(mesh):
    spec = P(("conv", "ctx"), "head", None)
    return jax.shard_map(
        per_device,
        mesh=mesh,
        in_specs=(spec,) * 5 + (P("conv"),),
        out_specs=spec,
        check_vma=False,
    )
```
